32 devices in a mesh: gx: 2 (over x), gy: 4 (over y, core), gz: 4 (over z).
Axes of the slice: x: 2, y: 2, z: 4, core: 2. Of those that a mesh axis runs over, the one named last changes fastest.
Arguments:
- panel: float32 [64, 16, 32, 512], P(None, 'gx', 'gy', 'gz')
- potential: float32 [16, 32, 512], P('gx', 'gy', 'gz'), may hold values from -10 to 10
- atom_corner: int32 [256, 3], P(('gx', 'gy', 'gz')), may hold values from 0 to 508, as said below
- proj_index: int32 [256, 64], P(('gx', 'gy', 'gz')), may hold values from 0 to 63, each once within a row
- projectors: float32 [256, 8, 64], P(('gx', 'gy', 'gz')), may hold values from -3 to 3
- couplings: float32 [256, 8], P(('gx', 'gy', 'gz')), may hold values from 0.5 to 8
Outputs:
- filtered: float32 [64, 16, 32, 512], P(None, 'gx', 'gy', 'gz')
- gram: float32 [64, 64], P('gz')
The draws below stay inside these ranges and needn't reach their ends.
Inputs may be any that keep to these rules, and one draw needn't show every extreme that they name: `atom_corner`: each atom's tile of 4 x 4 x 4 cells lies inside the domain of the device that holds the atom's row (rows of 8 atoms a device, devices in the order gx, gy, gz); tiles of different atoms may intersect.
All inputs are finite; a program needn't handle non-finite values.
Results may differ from the reference program's by a relative error of at most 0.0001.
Values sent between devices are 32-bit elements; how exact they have to be, the bound alone decides.
No kernel may reach another device: no remote copies, remote signals or barrier semaphores. Data moves between devices by JAX's collectives and lax.ppermute only.
A program may use at most 128 MiB of HBM per device.

```python
import math
import jax
import jax.numpy as jnp
from jax import lax

CX = 8
CY = 8
CZ = 128
ATOM_DEV = 8
BANDS = 64
NPROJ = 8
TILE = 64
DEGREE = 4
NX = 16
NY = 32
NZ = 512
ATOMS = 256
N_GY = 4
N_GZ = 4


def draw_panel(key, part):
    key = jax.random.fold_in(key, 1)
    coord = jnp.arange(NX, dtype=jnp.float32)
    scale_x = 0.5 + 1.5 * coord / max(NX - 1, 1)
    values = jax.random.normal(key, (BANDS, NX, NY, NZ), jnp.float32) * scale_x[None, :, None, None]
    return jnp.clip(values, -8.0, 8.0).astype(jnp.float32)


def draw_atom_corner(key, part):
    key = jax.random.fold_in(key, 2)
    owner = jnp.arange(ATOMS, dtype=jnp.int32) // ATOM_DEV
    pos_x = owner // (N_GY * N_GZ)
    pos_y = owner // N_GZ % N_GY
    pos_z = owner % N_GZ
    limits = jnp.array([CX - 3, CY - 3, CZ - 3], jnp.int32)
    local = jax.random.randint(key, (ATOMS, 3), 0, limits[None, :], jnp.int32)
    local = local.at[0].set(jnp.zeros((3,), jnp.int32))
    local = local.at[ATOMS - 1].set(limits - 1)
    anchor = jnp.stack([pos_x * CX, pos_y * CY, pos_z * CZ], axis=1)
    return (anchor + local).astype(jnp.int32)


def steps_of(stream_key, extent, pieces, smallest, largest):
    gain = 1.0
    for position, parts in pieces:
        steps = jax.random.uniform(jax.random.fold_in(jax.random.fold_in(stream_key, 6), position), (parts,), jnp.float32, smallest / len(pieces), largest / len(pieces))
        gain = gain * jnp.repeat(jnp.exp(steps), extent[position] // parts).reshape((-1,) + (1,) * (len(extent) - 1 - position))
    return gain


def centred(own_key, shape, width, bound, split=(), held_as=jnp.bfloat16):
    result = jax.random.normal(own_key, shape, jnp.float32) * width
    if len(split) > 0:
        result = steps_of(own_key, shape, split, -0.22, 0.18) * result
    return jnp.clip(result, min=-bound, max=bound).astype(held_as)


def setup_inputs(seed: int = 0) -> dict:
    seeds = jax.random.split(jax.random.key(seed), 7)
    panel = draw_panel(jax.random.fold_in(seeds[6], 71), 0)
    potential = jnp.clip(jax.random.uniform(seeds[1], (NX, NY, NZ), jnp.float32, -10.0, 10.0) * steps_of(seeds[1], (NX, NY, NZ), ((0, 2), (1, 4), (2, 4)), -0.4, 0.0), -10.0, 10.0)
    atom_corner = draw_atom_corner(jax.random.fold_in(seeds[6], 71), 0)
    proj_index = jax.vmap(lambda own: jax.random.permutation(own, TILE))(jax.random.split(seeds[3], ATOMS)).reshape((ATOMS, TILE)).astype(jnp.int32)
    projectors = centred(seeds[4], (ATOMS, NPROJ, TILE), 0.5, 3.0, ((0, 32),), jnp.float32)
    couplings = jnp.clip(jnp.exp(math.log(8.0) - 2.7725887 * jax.random.uniform(seeds[5], (ATOMS, NPROJ), jnp.float32) ** steps_of(seeds[5], (ATOMS, NPROJ), ((0, 32),), -0.2, 0.2)), 0.5, 8.0)
    return {"panel": panel, "potential": potential, "atom_corner": atom_corner, "proj_index": proj_index, "projectors": projectors, "couplings": couplings}


STENCIL = (-5369.0 / 1800.0, 12.0 / 7.0, -15.0 / 56.0, 10.0 / 189.0, -1.0 / 112.0, 2.0 / 1925.0, -1.0 / 16632.0)
SPACING = 0.224
CENTER = 210.5
HALF = 209.5


def tile_points(corner, order, size_y, size_z):
    off_x = order // 16
    off_y = (order // 4) % 4
    off_z = order % 4
    pos_x = corner[:, 0:1] + off_x
    pos_y = corner[:, 1:2] + off_y
    pos_z = corner[:, 2:3] + off_z
    return ((pos_x * size_y + pos_y) * size_z + pos_z).astype(jnp.int32)


def nonlocal_part(field, points, projectors, couplings):
    bands = field.shape[0]
    field_flat = field.reshape(bands, -1)
    taken = field_flat[:, points]
    coeffs = jnp.einsum("ajp,bap->baj", projectors, taken, precision=lax.Precision.HIGHEST) * couplings[None]
    spread = jnp.einsum("ajp,baj->bap", projectors, coeffs, precision=lax.Precision.HIGHEST)
    return jnp.zeros_like(field_flat).at[:, points].add(spread).reshape(field.shape)


def laplace(field):
    summed = 3.0 * STENCIL[0] * field
    for offset in range(1, 7):
        for axis_dim in (1, 2, 3):
            summed = summed + STENCIL[offset] * (jnp.roll(field, -offset, axis_dim) + jnp.roll(field, offset, axis_dim))
    return summed / (SPACING * SPACING)


def hamiltonian(field, potential, points, projectors, couplings):
    return -0.5 * laplace(field) + potential[None] * field + nonlocal_part(field, points, projectors, couplings)


def reference(panel, potential, atom_corner, proj_index, projectors, couplings):
    points = tile_points(atom_corner, proj_index, NY, NZ)
    previous = panel
    image = hamiltonian(panel, potential, points, projectors, couplings)
    current = (image - CENTER * panel) / HALF
    for degree_step in range(DEGREE - 1):
        image = hamiltonian(current, potential, points, projectors, couplings)
        following = 2.0 * (image - CENTER * current) / HALF - previous
        previous = current
        current = following
    field_flat = current.reshape(BANDS, -1)
    gram = jnp.einsum("bc,dc->bd", field_flat, field_flat, precision=lax.Precision.HIGHEST)
    return current, gram / (NX * NY * NZ)
```

```python
import functools
import math

import jax
import jax.numpy as jnp
import ml_dtypes
import numpy as np
from jax import lax
from jax.experimental import pallas as pl
from jax.experimental.pallas import tpu as pltpu
from jax.sharding import PartitionSpec as P

DEGREE = 4
CHUNKS = 2

STENCIL = (
    -5369.0 / 1800.0,
    12.0 / 7.0,
    -15.0 / 56.0,
    10.0 / 189.0,
    -1.0 / 112.0,
    2.0 / 1925.0,
    -1.0 / 16632.0,
)
SPACING = 0.224
CENTER = 210.5
HALF = 209.5
REACH = 6
TILE = 64
LANES = 128
SUBS = 8
KINETIC = -0.5 / (SPACING * SPACING) / HALF
TAPS = tuple(KINETIC * c for c in STENCIL)
DIAGONAL = 3.0 * TAPS[0] - CENTER / HALF

F32 = jnp.float32
BF16 = jnp.bfloat16
VMEM = pl.BlockSpec(memory_space=pltpu.VMEM)
SMEM = pl.BlockSpec(memory_space=pltpu.SMEM)
ANY = pl.BlockSpec(memory_space=pl.ANY)


def split_halves(matrix):
    high = matrix.astype(ml_dtypes.bfloat16)
    low = (matrix - high.astype(np.float64)).astype(ml_dtypes.bfloat16)
    wide = np.concatenate([high, low], axis=1)
    return np.concatenate([wide, wide], axis=0)


def line_weights():
    own = np.zeros((LANES, LANES))
    halo = np.zeros((LANES, LANES))
    for k in range(1, REACH + 1):
        for z in range(LANES):
            if z + k < LANES:
                own[z + k, z] = TAPS[k]
            else:
                halo[8 + z + k - LANES, z] = TAPS[k]
            if z - k >= 0:
                own[z - k, z] = TAPS[k]
            else:
                halo[REACH + z - k, z] = TAPS[k]
    return np.concatenate([split_halves(own), split_halves(halo)], axis=0)


def halves(value):
    high = value.astype(BF16)
    low = (value - high.astype(F32)).astype(BF16)
    return high, low


def parts_kernel(count, index_ref, proj_ref, root_ref, pot_ref, meta_ref, out_ref):
    out_ref[0:64, :] = pot_ref[...]
    point = lax.broadcasted_iota(jnp.int32, (TILE, TILE), 0)
    for pair in range(count // 2):
        both = []
        for atom in (2 * pair, 2 * pair + 1):
            order = index_ref[atom : atom + 1, :]
            hot = (point == order).astype(F32)
            both.append(
                lax.dot_general(
                    proj_ref[atom],
                    hot,
                    (((1,), (1,)), ((), ())),
                    precision=lax.Precision.HIGHEST,
                    preferred_element_type=F32,
                )
                * root_ref[:, atom : atom + 1]
            )
        out_ref[64 + 8 * pair : 72 + 8 * pair, :] = jnp.concatenate(both, axis=1)
    out_ref[64 + 4 * count : 72 + 4 * count, :] = meta_ref[...]


def setup_kernel(gx, gy, nb, count, me_ref, *refs):
    group = gx * gy
    blocks = refs[:group]
    diag_ref, q_ref, meta_ref, pots, roots, raw, sem = refs[group:]
    rows = 4 * count
    copies = []
    for d in range(group):
        slot = me_ref[0] ^ d
        i, j = slot // gy, slot % gy
        for b in range(nb):
            copies.append(
                pltpu.make_async_copy(
                    blocks[d].at[pl.ds(0, 64)],
                    pots.at[pl.ds(pl.multiple_of(((j * gx + i) * nb + b) * 64, 64), 64)],
                    sem.at[0],
                )
            )
        copies.append(
            pltpu.make_async_copy(
                blocks[d].at[pl.ds(64, rows)],
                roots.at[pl.ds(pl.multiple_of(slot * rows, 8), rows)],
                sem.at[0],
            )
        )
        copies.append(
            pltpu.make_async_copy(
                blocks[d].at[pl.ds(64 + rows, 8)],
                raw.at[pl.ds(pl.multiple_of(slot * 8, 8), 8)],
                sem.at[0],
            )
        )
    for copy in copies:
        copy.start()
    for copy in copies:
        copy.wait()

    def corner(n, carry):
        slot = n // count
        atom = n % count
        base = raw[slot * 8, atom].astype(jnp.int32)
        meta_ref[2 * n] = base + (slot % gy) * 64
        meta_ref[2 * n + 1] = raw[slot * 8, count + atom].astype(jnp.int32)
        return carry

    lax.fori_loop(0, group * count, corner, 0)

    def line(y, carry):
        for x in range(8):
            start = (y // 8) * 512 + y % 8 + x * 8
            value = pots[pl.ds(start, SUBS, stride=64), :]
            diag_ref[y * 8 + x] = value * (1.0 / HALF) + DIAGONAL
        return carry

    lax.fori_loop(0, gy * 8, line, 0)
    same = lax.broadcasted_iota(jnp.int32, (LANES, LANES), 0) // TILE == (
        lax.broadcasted_iota(jnp.int32, (LANES, LANES), 1) // TILE
    )

    def pair(p, carry):
        root = roots[pl.ds(pl.multiple_of(p * 8, 8), 8), :]
        full = lax.dot_general(
            root,
            root,
            (((0,), (0,)), ((), ())),
            precision=lax.Precision.HIGHEST,
            preferred_element_type=F32,
        )
        high, low = halves(jnp.where(same, full, 0.0))
        q_ref[p] = jnp.concatenate([high, low], axis=1)
        return carry

    lax.fori_loop(0, group * count // 2, pair, 0)


def pack_edges(values, lane):
    low = high = None
    for slot, value in enumerate(values):
        here = (lane >> 3) == slot
        to_low = pltpu.roll(value, 8 * slot, 1) if slot else value
        to_high = pltpu.roll(value, (8 * slot - (LANES - REACH)) % LANES, 1)
        low = to_low if low is None else jnp.where(here, to_low, low)
        high = to_high if high is None else jnp.where(here, to_high, high)
    return low, high


def unpack_kernel(gx, gy, nb, me_ref, *refs):
    group = gx * gy
    blocks = refs[:group]
    z_ref, low_ref, high_ref, staged, sem = refs[group:]
    size = nb * 64
    copies = []
    for d in range(group):
        slot = me_ref[0] ^ d
        i, j = slot // gy, slot % gy
        copies.append(
            pltpu.make_async_copy(
                blocks[d],
                staged.at[pl.ds(pl.multiple_of((j * gx + i) * size, 64), size)],
                sem.at[0],
            )
        )
    for copy in copies:
        copy.start()
    for copy in copies:
        copy.wait()
    lane = lax.broadcasted_iota(jnp.int32, (SUBS, LANES), 1)

    def lines(pair, carry):
        values = []
        for q in range(2):
            y = 2 * pair + q
            for x in range(8):
                start = (y // 8) * 512 + y % 8 + x * 8
                value = staged[pl.ds(start, SUBS, stride=64), :]
                z_ref[y * 8 + x] = value
                values.append(value)
        low, high = pack_edges(values, lane)
        low_ref[pair] = low
        high_ref[pair] = high
        return carry

    lax.fori_loop(0, gy * 4, lines, 0)


def step_kernel(gx, gy, nb, count, first, last, me_ref, meta_ref, *refs):
    group = gx * gy
    if first:
        z_ref, diag_ref, q_ref, below_ref, above_ref, w_ref = refs[:6]
        refs = refs[6:]
    else:
        z_ref, prev_ref, diag_ref, q_ref, below_ref, above_ref, w_ref = refs[:7]
        refs = refs[7:]
    if last:
        blocks = refs[:group]
        acc, out_ref, sem = refs[group:]
    else:
        out_ref, low_ref, high_ref, acc = refs
    ny = gy * 8
    lane = lax.broadcasted_iota(jnp.int32, (SUBS, LANES), 1)
    row_part = lax.broadcasted_iota(jnp.int32, (SUBS, LANES), 0) // nb

    def second_dim(x, carry):
        values = [z_ref[y * 8 + x] for y in range(ny)]
        for y in range(ny):
            total = None
            for k in range(1, REACH + 1):
                term = TAPS[k] * (values[(y + k) % ny] + values[(y - k) % ny])
                total = term if total is None else total + term
            acc[y * 8 + x] = total
        return carry

    lax.fori_loop(0, 8, second_dim, 0)

    def atoms(slot, carry):
        part = slot // gy
        places = []
        tiles = []
        for p in range(count // 2):
            tile = jnp.zeros((SUBS, LANES), F32)
            for q in range(2):
                n = slot * count + 2 * p + q
                base = meta_ref[2 * n]
                z0 = meta_ref[2 * n + 1]
                places.append((base, z0))
                for t in range(16):
                    value = z_ref[base + (t % 4) * 8 + t // 4]
                    shifted = pltpu.roll(value, (4 * t + TILE * q - z0 + LANES) & (LANES - 1), 1)
                    tile = jnp.where((lane >> 2) == t + 16 * q, shifted, tile)
            tiles.append(tile)
        spreads = []
        for p in range(count // 2):
            high, low = halves(tiles[p])
            product = jnp.dot(
                jnp.concatenate([high, low], axis=0),
                q_ref[slot * (count // 2) + p],
                preferred_element_type=F32,
            )
            spreads.append(
                product[:SUBS, :LANES]
                + product[:SUBS, LANES:]
                + product[SUBS:, :LANES]
                + product[SUBS:, LANES:]
            )
        for n in range(count):
            base, z0 = places[n]
            inside = (row_part == part) & (lane >= z0) & (lane < z0 + 4)
            for t in range(16):
                shifted = pltpu.roll(
                    spreads[n // 2], (z0 - 4 * t - TILE * (n % 2) + LANES) & (LANES - 1), 1
                )
                row = base + (t % 4) * 8 + t // 4
                acc[row] = acc[row] + jnp.where(inside, shifted, 0.0)
        return carry

    lax.fori_loop(0, group, atoms, 0)

    def rest(four, carry):
        tiles = z_ref[pl.ds(four * 32, 32)]
        own = tiles.reshape(32 * SUBS, LANES)
        joined = []
        for q in range(2):
            below = below_ref[2 * four + q]
            above = above_ref[2 * four + q]
            for slot in range(16):
                left = pltpu.roll(below, (-8 * slot) % LANES, 1)
                right = pltpu.roll(above, (8 - 8 * slot) % LANES, 1)
                joined.append(jnp.where(lane < 8, left, right))
        halo = jnp.concatenate(joined, axis=0)
        operand = jnp.concatenate([*halves(own), *halves(halo)], axis=1)
        product = jnp.dot(operand, w_ref[...], preferred_element_type=F32)
        third = (product[:, :LANES] + product[:, LANES:]).reshape(32, SUBS, LANES)
        results = []
        for q in range(4):
            values = [tiles[8 * q + x] for x in range(8)]
            after = [pltpu.roll(value, SUBS - nb, 0) for value in values]
            before = after if gx == 2 else [pltpu.roll(value, nb, 0) for value in values]
            wide = before + values + after
            for x in range(8):
                total = acc[four * 32 + 8 * q + x] + third[8 * q + x]
                total = total + diag_ref[four * 32 + 8 * q + x] * values[x]
                for k in range(1, REACH + 1):
                    total = total + TAPS[k] * (wide[8 + x + k] + wide[8 + x - k])
                if not first:
                    total = 2.0 * total - prev_ref[four * 32 + 8 * q + x]
                results.append(total)
                if last:
                    y = four * 4 + q
                    start = (y // 8) * 512 + y % 8 + x * 8
                    out_ref[pl.ds(start, SUBS, stride=64), :] = total
                else:
                    out_ref[four * 32 + 8 * q + x] = total
        if not last:
            for q in range(2):
                low, high = pack_edges(results[16 * q : 16 * q + 16], lane)
                low_ref[2 * four + q] = low
                high_ref[2 * four + q] = high
        return carry

    lax.fori_loop(0, gy * 2, rest, 0)
    if last:
        size = nb * 64
        copies = []
        for d in range(group):
            slot = me_ref[0] ^ d
            i, j = slot // gy, slot % gy
            copies.append(
                pltpu.make_async_copy(
                    out_ref.at[pl.ds(pl.multiple_of((j * gx + i) * size, 64), size)],
                    blocks[d],
                    sem.at[0],
                )
            )
        for copy in copies:
            copy.start()
        for copy in copies:
            copy.wait()


def gather_kernel(group, nb, bands, me_ref, *refs):
    blocks = refs[: CHUNKS * group]
    out_ref, gram_ref, field, sem = refs[CHUNKS * group :]
    size = nb * 64
    copies = []
    for chunk in range(CHUNKS):
        for d in range(group):
            slot = me_ref[0] ^ d
            row = (chunk * group + slot) * size
            copies.append(
                pltpu.make_async_copy(
                    blocks[chunk * group + d],
                    field.at[pl.ds(pl.multiple_of(row, 64), size)],
                    sem.at[0],
                )
            )
    for copy in copies:
        copy.start()
    for copy in copies:
        copy.wait()
    store = pltpu.make_async_copy(field, out_ref, sem.at[0])
    store.start()
    gram_ref[...] = jnp.zeros_like(gram_ref)

    def cells(n, carry):
        total = None
        for m in range(4):
            pieces = []
            for c in range(2):
                cell = n * 8 + m * 2 + c
                pieces.append(
                    jnp.concatenate(
                        [
                            field[pl.ds(g * SUBS * 64 + cell, SUBS, stride=64), :]
                            for g in range(bands // SUBS)
                        ],
                        axis=0,
                    )
                )
            value = jnp.concatenate(pieces, axis=1)
            high, low = halves(value)
            both = jnp.concatenate([high, low], axis=0)
            product = lax.dot_general(
                both, both, (((1,), (1,)), ((), ())), preferred_element_type=F32
            )
            total = product if total is None else total + product
        gram_ref[...] += (
            total[:bands, :bands]
            + total[bands:, :bands]
            + total[:bands, bands:]
            + total[bands:, bands:]
        )
        return carry

    lax.fori_loop(0, 8, cells, 0)
    store.wait()


def shape(*dims, dtype=F32):
    return jax.ShapeDtypeStruct(dims, dtype)


def shards(panel, potential, atom_corner, proj_index, projectors, couplings):
    bands, size_x, size_y, size_z = panel.shape
    count, nproj = couplings.shape
    gx, gy, gz = lax.axis_size("gx"), lax.axis_size("gy"), lax.axis_size("gz")
    group = gx * gy
    nb = bands // (CHUNKS * group)
    column = ("gx", "gy")
    me = lax.axis_index("gx") * gy + lax.axis_index("gy")
    me_arr = me.reshape(1)
    rows = gy * 64
    pairs = gy * 4

    def swap(block, d):
        return lax.ppermute(block, column, [(s, s ^ d) for s in range(group)])

    anchor = jnp.stack(
        [
            lax.axis_index("gx") * size_x,
            lax.axis_index("gy") * size_y,
            lax.axis_index("gz") * size_z,
        ]
    )
    local = atom_corner - anchor[None, :]
    meta = jnp.concatenate([local[:, 1] * 8 + local[:, 0], local[:, 2]]).astype(F32)
    meta = jnp.broadcast_to(jnp.pad(meta, (0, LANES - 2 * count))[None], (8, LANES))
    part_rows = 64 + 4 * count + 8
    parts = pl.pallas_call(
        functools.partial(parts_kernel, count),
        out_shape=shape(part_rows, LANES),
        in_specs=[VMEM] * 5,
        out_specs=VMEM,
        name="parts",
    )(
        proj_index,
        projectors,
        jnp.sqrt(couplings * (1.0 / HALF)).T,
        potential.reshape(64, LANES),
        meta,
    )
    others = [parts] + [swap(parts, d) for d in range(1, group)]

    field = panel.reshape(bands * 64, LANES)
    size = nb * 64
    forward = []
    for chunk in range(CHUNKS):
        own = [
            lax.dynamic_slice_in_dim(field, (chunk * group + (me ^ d)) * size, size, 0)
            for d in range(group)
        ]
        forward.append([own[0]] + [swap(own[d], d) for d in range(1, group)])

    diag, q_mat, places = pl.pallas_call(
        functools.partial(setup_kernel, gx, gy, nb, count),
        out_shape=[
            shape(rows, SUBS, LANES),
            shape(group * count // 2, LANES, 2 * LANES, dtype=BF16),
            shape(2 * group * count, dtype=jnp.int32),
        ],
        in_specs=[SMEM] + [ANY] * group,
        out_specs=[VMEM, VMEM, SMEM],
        scratch_shapes=[
            pltpu.VMEM((rows * SUBS, LANES), F32),
            pltpu.VMEM((group * 4 * count, LANES), F32),
            pltpu.SMEM((group * 8, LANES), F32),
            pltpu.SemaphoreType.DMA((1,)),
        ],
        name="setup",
    )(me_arr, *others)

    weights = jnp.asarray(line_weights())
    up = [(s, (s + 1) % gz) for s in range(gz)]
    down = [(s, (s - 1) % gz) for s in range(gz)]

    def halos(low, high):
        return lax.ppermute(high, "gz", up), lax.ppermute(low, "gz", down)

    tile_shape = shape(rows, SUBS, LANES)
    edge_shape = shape(pairs, SUBS, LANES)
    states = []
    for chunk in range(CHUNKS):
        tiles, low, high = pl.pallas_call(
            functools.partial(unpack_kernel, gx, gy, nb),
            out_shape=[tile_shape, edge_shape, edge_shape],
            in_specs=[SMEM] + [ANY] * group,
            out_specs=[VMEM] * 3,
            scratch_shapes=[
                pltpu.VMEM((rows * SUBS, LANES), F32),
                pltpu.SemaphoreType.DMA((1,)),
            ],
            name="unpack",
        )(me_arr, *forward[chunk])
        states.append((None, tiles, low, high))

    cost = pl.CostEstimate(flops=rows * SUBS * LANES * 2000, bytes_accessed=8 << 20, transcendentals=0)
    results = [None] * CHUNKS
    for degree_step in range(DEGREE):
        first, last = degree_step == 0, degree_step == DEGREE - 1
        for chunk in range(CHUNKS):
            prev, tiles, low, high = states[chunk]
            below, above = halos(low, high)
            operands = [me_arr, places, tiles]
            if not first:
                operands.append(prev)
            operands += [diag, q_mat, below, above, weights]
            scratch = [pltpu.VMEM((rows, SUBS, LANES), F32)]
            if last:
                out_shape = [shape(size, LANES)] * group
                out_specs = [ANY] * group
                scratch += [
                    pltpu.VMEM((rows * SUBS, LANES), F32),
                    pltpu.SemaphoreType.DMA((1,)),
                ]
            else:
                out_shape = [tile_shape, edge_shape, edge_shape]
                out_specs = [VMEM] * 3
            outs = pl.pallas_call(
                functools.partial(step_kernel, gx, gy, nb, count, first, last),
                out_shape=out_shape,
                in_specs=[SMEM, SMEM] + [VMEM] * (len(operands) - 2),
                out_specs=out_specs,
                scratch_shapes=scratch,
                compiler_params=pltpu.CompilerParams(vmem_limit_bytes=24 << 20),
                cost_estimate=cost,
                name="step",
            )(*operands)
            if last:
                results[chunk] = [outs[0]] + [swap(outs[d], d) for d in range(1, group)]
            else:
                states[chunk] = (tiles, *outs)

    filtered, gram = pl.pallas_call(
        functools.partial(gather_kernel, group, nb, bands),
        out_shape=[shape(bands * 64, LANES), shape(bands, bands)],
        in_specs=[SMEM] + [ANY] * (CHUNKS * group),
        out_specs=[ANY, VMEM],
        scratch_shapes=[
            pltpu.VMEM((bands * 64, LANES), F32),
            pltpu.SemaphoreType.DMA((1,)),
        ],
        name="gather",
    )(me_arr, *[block for chunk in results for block in chunk])

    d = 1
    while d < group:
        gram = gram + swap(gram, d)
        d *= 2
    d = 1
    while d < gz:
        gram = gram + lax.ppermute(gram, "gz", [(s, s ^ d) for s in range(gz)])
        d *= 2
    total_cells = size_x * size_y * size_z * group * gz
    share = bands // gz
    gram = lax.dynamic_slice_in_dim(gram, lax.axis_index("gz") * share, share, 0)
    return filtered.reshape(panel.shape), gram * (1.0 / total_cells)


def solution(mesh):
    placed = (
        P(None, "gx", "gy", "gz"),
        P("gx", "gy", "gz"),
        P(("gx", "gy", "gz"), None),
        P(("gx", "gy", "gz"), None),
        P(("gx", "gy", "gz"), None, None),
        P(("gx", "gy", "gz"), None),
    )
    return jax.shard_map(
        shards,
        mesh=mesh,
        in_specs=placed,
        out_specs=(P(None, "gx", "gy", "gz"), P("gz", None)),
        check_vma=False,
    )
```

```python
import functools
import math

import jax
import jax.numpy as jnp
import ml_dtypes
import numpy as np
from jax import lax
from jax.experimental import pallas as pl
from jax.experimental.pallas import tpu as pltpu
from jax.sharding import PartitionSpec as P

DEGREE = 4
CHUNKS = 2

STENCIL = (
    -5369.0 / 1800.0,
    12.0 / 7.0,
    -15.0 / 56.0,
    10.0 / 189.0,
    -1.0 / 112.0,
    2.0 / 1925.0,
    -1.0 / 16632.0,
)
SPACING = 0.224
CENTER = 210.5
HALF = 209.5
REACH = 6
TILE = 64
LANES = 128
SUBS = 8
KINETIC = -0.5 / (SPACING * SPACING) / HALF
TAPS = tuple(KINETIC * c for c in STENCIL)
DIAGONAL = 3.0 * TAPS[0] - CENTER / HALF

F32 = jnp.float32
BF16 = jnp.bfloat16
VMEM = pl.BlockSpec(memory_space=pltpu.VMEM)
SMEM = pl.BlockSpec(memory_space=pltpu.SMEM)
ANY = pl.BlockSpec(memory_space=pl.ANY)


def split_halves(matrix):
    high = matrix.astype(ml_dtypes.bfloat16)
    low = (matrix - high.astype(np.float64)).astype(ml_dtypes.bfloat16)
    wide = np.concatenate([high, low], axis=1)
    return np.concatenate([wide, wide], axis=0)


def line_weights():
    own = np.zeros((LANES, LANES))
    halo = np.zeros((LANES, LANES))
    for k in range(1, REACH + 1):
        for z in range(LANES):
            if z + k < LANES:
                own[z + k, z] = TAPS[k]
            else:
                halo[8 + z + k - LANES, z] = TAPS[k]
            if z - k >= 0:
                own[z - k, z] = TAPS[k]
            else:
                halo[REACH + z - k, z] = TAPS[k]
    return np.concatenate([split_halves(own), split_halves(halo)], axis=0)


def halves(value):
    high = value.astype(BF16)
    low = (value - high.astype(F32)).astype(BF16)
    return high, low


def parts_kernel(count, fold, index_ref, proj_ref, root_ref, pot_ref, meta_ref, out_ref):
    out_ref[0:64, :] = pot_ref[...]
    point = lax.broadcasted_iota(jnp.int32, (TILE, TILE), 0)
    width = TILE // fold
    sorted_rows = []
    for atom in range(count):
        order = index_ref[atom : atom + 1, :]
        if fold == 2:
            order = ((order >> 4) & 1) * width + (order >> 5) * 16 + (order & 15)
        hot = (point == order).astype(F32)
        sorted_rows.append(
            lax.dot_general(
                proj_ref[atom],
                hot,
                (((1,), (1,)), ((), ())),
                precision=lax.Precision.HIGHEST,
                preferred_element_type=F32,
            )
            * root_ref[:, atom : atom + 1]
        )
    row = 64
    for first in range(0, count, 2 * fold):
        for f in range(fold):
            out_ref[row : row + 8, :] = jnp.concatenate(
                [sorted_rows[first + q][:, f * width : (f + 1) * width] for q in range(2 * fold)],
                axis=1,
            )
            row += 8
    out_ref[row : row + 8, :] = meta_ref[...]


def setup_kernel(gx, gy, nb, count, fold, me_ref, *refs):
    group = gx * gy
    blocks = refs[:group]
    diag_ref, roots_ref, meta_ref, pots, roots, raw, sem = refs[group:]
    rows = 4 * count
    copies = []
    for d in range(group):
        slot = me_ref[0] ^ d
        i, j = slot // gy, slot % gy
        for b in range(nb):
            copies.append(
                pltpu.make_async_copy(
                    blocks[d].at[pl.ds(0, 64)],
                    pots.at[pl.ds(pl.multiple_of(((j * gx + i) * nb + b) * 64, 64), 64)],
                    sem.at[0],
                )
            )
        copies.append(
            pltpu.make_async_copy(
                blocks[d].at[pl.ds(64, rows)],
                roots.at[pl.ds(pl.multiple_of(slot * rows, 8), rows)],
                sem.at[0],
            )
        )
        copies.append(
            pltpu.make_async_copy(
                blocks[d].at[pl.ds(64 + rows, 8)],
                raw.at[pl.ds(pl.multiple_of(slot * 8, 8), 8)],
                sem.at[0],
            )
        )
    for copy in copies:
        copy.start()
    for copy in copies:
        copy.wait()

    def corners(slot, carry):
        for atom in range(count):
            n = slot * count + atom
            meta_ref[2 * n] = raw[slot * 8, atom].astype(jnp.int32) + (slot % gy) * 64
            meta_ref[2 * n + 1] = raw[slot * 8, count + atom].astype(jnp.int32)
        return carry

    lax.fori_loop(0, group, corners, 0)

    def lines(j, carry):
        for y in range(8):
            for x in range(8):
                value = pots[pl.ds(j * 512 + x * 8 + y, SUBS, stride=64), :]
                diag_ref[(j * 8 + y) * 8 + x] = value * (1.0 / HALF) + DIAGONAL
        return carry

    lax.fori_loop(0, gy, lines, 0)
    sub = lax.broadcasted_iota(jnp.int32, (SUBS, LANES), 0)

    def spread(m, carry):
        for k in range(8):
            parts = [
                jnp.broadcast_to(roots[pl.ds(m * 8 * fold + f * 8 + k, 1), :], (SUBS, LANES))
                for f in range(fold)
            ]
            value = parts[0] if fold == 1 else jnp.where(sub < SUBS // 2, parts[0], parts[1])
            roots_ref[m * 8 + k] = value
        return carry

    lax.fori_loop(0, group * count // (2 * fold), spread, 0)


def pack_edges(values, lane):
    low = high = None
    for slot, value in enumerate(values):
        here = (lane >> 3) == slot
        to_low = pltpu.roll(value, 8 * slot, 1) if slot else value
        to_high = pltpu.roll(value, (8 * slot - (LANES - REACH)) % LANES, 1)
        low = to_low if low is None else jnp.where(here, to_low, low)
        high = to_high if high is None else jnp.where(here, to_high, high)
    return low, high


def send_edges(even, low, high):
    return jnp.where(even, high, low), jnp.where(even, low, high)


def unpack_kernel(gx, gy, nb, me_ref, places_ref, *refs):
    group = gx * gy
    blocks = refs[:group]
    z_ref, one_ref, two_ref, staged, sem = refs[group:]
    size = nb * 64
    copies = []
    for d in range(group):
        slot = me_ref[0] ^ d
        i, j = slot // gy, slot % gy
        copies.append(
            pltpu.make_async_copy(
                blocks[d],
                staged.at[pl.ds(pl.multiple_of((j * gx + i) * size, 64), size)],
                sem.at[0],
            )
        )
    for copy in copies:
        copy.start()
    for copy in copies:
        copy.wait()
    lane = lax.broadcasted_iota(jnp.int32, (SUBS, LANES), 1)
    even = me_ref[1] == 0

    def lines(j, carry):
        for pair in range(4):
            values = []
            for q in range(2):
                y = 2 * pair + q
                for x in range(8):
                    value = staged[pl.ds(j * 512 + x * 8 + y, SUBS, stride=64), :]
                    z_ref[pl.ds(((j * 8 + y) * 8 + x) * SUBS, SUBS)] = value
                    values.append(value)
            low, high = pack_edges(values, lane)
            one_ref[j * 4 + pair], two_ref[j * 4 + pair] = send_edges(even, low, high)
        return carry

    lax.fori_loop(0, gy, lines, 0)


def step_kernel(gx, gy, nb, count, fold, first, last, me_ref, meta_ref, *refs):
    group = gx * gy
    if first:
        z_ref, diag_ref, roots_ref, one_in, two_in, w_ref, sum_ref = refs[:7]
        refs = refs[7:]
    else:
        z_ref, prev_ref, diag_ref, roots_ref, one_in, two_in, w_ref, sum_ref = refs[:8]
        refs = refs[8:]
    if last:
        blocks = refs[:group]
        acc, out_ref, sem = refs[group:]
    else:
        out_ref, one_ref, two_ref, acc = refs
    ny = gy * 8
    lane = lax.broadcasted_iota(jnp.int32, (SUBS, LANES), 1)
    sub = lax.broadcasted_iota(jnp.int32, (SUBS, LANES), 0)
    even = me_ref[1] == 0

    def tile_rows(row):
        return pl.ds(pl.multiple_of(row * SUBS, SUBS), SUBS)

    def second_dim(x, carry):
        values = [z_ref[tile_rows(y * 8 + x)] for y in range(ny)]
        for y in range(ny):
            total = None
            for k in range(1, REACH + 1):
                term = TAPS[k] * (values[(y + k) % ny] + values[(y - k) % ny])
                total = term if total is None else total + term
            acc[tile_rows(y * 8 + x)] = total
        return carry

    lax.fori_loop(0, 8, second_dim, 0)

    width = TILE // fold
    per_tile = 2 * fold

    def atoms(i, carry):
        places = []
        tiles = []
        for j in range(gy):
            for m in range(count // per_tile):
                tile = jnp.zeros((SUBS, LANES), F32)
                for q in range(per_tile):
                    n = (i * gy + j) * count + per_tile * m + q
                    base = meta_ref[2 * n]
                    z0 = meta_ref[2 * n + 1]
                    places.append((base, z0))
                    for t in range(16 // fold):
                        row = base + (t % 4) * 8 + (t // 4) * fold
                        if fold == 1:
                            value = z_ref[tile_rows(row)]
                        else:
                            start = row * SUBS + i * nb
                            value = jnp.where(
                                sub < nb,
                                z_ref[pl.ds(start, SUBS)],
                                z_ref[pl.ds(start + nb, SUBS)],
                            )
                        value = pltpu.roll(
                            value, (4 * t + width * q - z0 + LANES) & (LANES - 1), 1
                        )
                        tile = jnp.where((lane >> 2) == t + q * (width // 4), value, tile)
                tiles.append(tile)
        n_tiles = len(tiles)
        products = []
        for m in range(n_tiles):
            for k in range(8):
                products.append(tiles[m] * roots_ref[(i * n_tiles + m) * 8 + k])
        stacked = jnp.concatenate(products, axis=0)
        sums = jnp.dot(
            jnp.concatenate(halves(stacked), axis=1), sum_ref[...], preferred_element_type=F32
        )
        for m in range(n_tiles):
            spread = None
            for k in range(8):
                at = (m * 8 + k) * SUBS
                coeff = sums[at : at + SUBS]
                if fold == 2:
                    coeff = coeff + pltpu.roll(coeff, nb, 0)
                term = coeff * roots_ref[(i * n_tiles + m) * 8 + k]
                spread = term if spread is None else spread + term
            for q in range(per_tile):
                base, z0 = places[m * per_tile + q]
                inside = (lane >= z0) & (lane < z0 + 4)
                if fold == 1:
                    inside = inside & (sub // nb == i)
                for t in range(16 // fold):
                    row = base + (t % 4) * 8 + (t // 4) * fold
                    value = pltpu.roll(
                        spread, (z0 - 4 * t - width * q + LANES) & (LANES - 1), 1
                    )
                    value = jnp.where(inside, value, 0.0)
                    if fold == 1:
                        acc[tile_rows(row)] += value
                    else:
                        start = row * SUBS + i * nb
                        acc[pl.ds(start, SUBS)] += jnp.where(sub < nb, value, 0.0)
                        acc[pl.ds(start + nb, SUBS)] += jnp.where(sub < nb, 0.0, value)
        return carry

    lax.fori_loop(0, gx, atoms, 0)

    def rest(four, carry):
        own = z_ref[pl.ds(pl.multiple_of(four * 32 * SUBS, 32 * SUBS), 32 * SUBS)]
        joined = []
        for q in range(2):
            one = one_in[2 * four + q]
            two = two_in[2 * four + q]
            below = jnp.where(even, two, one)
            above = jnp.where(even, one, two)
            for slot in range(16):
                left = pltpu.roll(below, (-8 * slot) % LANES, 1)
                right = pltpu.roll(above, (8 - 8 * slot) % LANES, 1)
                joined.append(jnp.where(lane < 8, left, right))
        halo = jnp.concatenate(joined, axis=0)
        operand = jnp.concatenate([*halves(own), *halves(halo)], axis=1)
        product = jnp.dot(operand, w_ref[...], preferred_element_type=F32)
        third = product[:, :LANES] + product[:, LANES:]
        results = []
        for q in range(4):
            values = [own[(8 * q + x) * SUBS : (8 * q + x + 1) * SUBS] for x in range(8)]
            after = [pltpu.roll(value, SUBS - nb, 0) for value in values]
            before = after if gx == 2 else [pltpu.roll(value, nb, 0) for value in values]
            wide = before + values + after
            for x in range(8):
                at = 8 * q + x
                here = tile_rows(four * 32 + at)
                total = acc[here] + third[at * SUBS : (at + 1) * SUBS]
                total = total + diag_ref[four * 32 + at] * values[x]
                for k in range(1, REACH + 1):
                    total = total + TAPS[k] * (wide[8 + x + k] + wide[8 + x - k])
                if not first:
                    total = 2.0 * total - prev_ref[here]
                results.append(total)
                if last:
                    y = four * 4 + q
                    start = (y // 8) * 512 + y % 8 + x * 8
                    out_ref[pl.ds(start, SUBS, stride=64), :] = total
                else:
                    out_ref[here] = total
        if not last:
            for q in range(2):
                low, high = pack_edges(results[16 * q : 16 * q + 16], lane)
                one_ref[2 * four + q], two_ref[2 * four + q] = send_edges(even, low, high)
        return carry

    lax.fori_loop(0, gy * 2, rest, 0, unroll=2)
    if last:
        size = nb * 64
        copies = []
        for d in range(group):
            slot = me_ref[0] ^ d
            i, j = slot // gy, slot % gy
            copies.append(
                pltpu.make_async_copy(
                    out_ref.at[pl.ds(pl.multiple_of((j * gx + i) * size, 64), size)],
                    blocks[d],
                    sem.at[0],
                )
            )
        for copy in copies:
            copy.start()
        for copy in copies:
            copy.wait()


def gather_kernel(group, nb, bands, me_ref, *refs):
    blocks = refs[: CHUNKS * group]
    out_ref, gram_ref, field, sem = refs[CHUNKS * group :]
    size = nb * 64
    copies = []
    for chunk in range(CHUNKS):
        for d in range(group):
            slot = me_ref[0] ^ d
            row = (chunk * group + slot) * size
            copies.append(
                pltpu.make_async_copy(
                    blocks[chunk * group + d],
                    field.at[pl.ds(pl.multiple_of(row, 64), size)],
                    sem.at[0],
                )
            )
    for copy in copies:
        copy.start()
    for copy in copies:
        copy.wait()
    store = pltpu.make_async_copy(field, out_ref, sem.at[0])
    store.start()
    gram_ref[...] = jnp.zeros_like(gram_ref)

    def cells(n, carry):
        total = None
        for m in range(4):
            pieces = []
            for c in range(2):
                cell = n * 8 + m * 2 + c
                pieces.append(
                    jnp.concatenate(
                        [
                            field[pl.ds(g * SUBS * 64 + cell, SUBS, stride=64), :]
                            for g in range(bands // SUBS)
                        ],
                        axis=0,
                    )
                )
            value = jnp.concatenate(pieces, axis=1)
            high, low = halves(value)
            both = jnp.concatenate([high, low], axis=0)
            product = lax.dot_general(
                both, both, (((1,), (1,)), ((), ())), preferred_element_type=F32
            )
            total = product if total is None else total + product
        gram_ref[...] += (
            total[:bands, :bands]
            + total[bands:, :bands]
            + total[:bands, bands:]
            + total[bands:, bands:]
        )
        return carry

    lax.fori_loop(0, 8, cells, 0)
    store.wait()


def shape(*dims, dtype=F32):
    return jax.ShapeDtypeStruct(dims, dtype)


def cost(microseconds):
    return pl.CostEstimate(
        flops=int(microseconds * 1e9), bytes_accessed=int(microseconds * 3e6), transcendentals=0
    )


def shards(panel, potential, atom_corner, proj_index, projectors, couplings):
    bands, size_x, size_y, size_z = panel.shape
    count, nproj = couplings.shape
    gx, gy, gz = lax.axis_size("gx"), lax.axis_size("gy"), lax.axis_size("gz")
    group = gx * gy
    nb = bands // (CHUNKS * group)
    fold = 2 if gx == 2 else 1
    column = ("gx", "gy")
    me = lax.axis_index("gx") * gy + lax.axis_index("gy")
    me_z = lax.axis_index("gz")
    me_arr = jnp.stack([me, me_z % 2])
    rows = gy * 64
    pairs = gy * 4

    def swap(block, d):
        return lax.ppermute(block, column, [(s, s ^ d) for s in range(group)])

    def swap_z(block, d):
        return lax.ppermute(block, "gz", [(s, s ^ d) for s in range(gz)])

    anchor = jnp.stack(
        [
            lax.axis_index("gx") * size_x,
            lax.axis_index("gy") * size_y,
            me_z * size_z,
        ]
    )
    local = atom_corner - anchor[None, :]
    meta = jnp.concatenate([local[:, 1] * 8 + local[:, 0], local[:, 2]]).astype(F32)
    meta = jnp.broadcast_to(jnp.pad(meta, (0, LANES - 2 * count))[None], (8, LANES))
    part_rows = 64 + 4 * count + 8
    parts = pl.pallas_call(
        functools.partial(parts_kernel, count, fold),
        out_shape=shape(part_rows, LANES),
        in_specs=[VMEM] * 5,
        out_specs=VMEM,
        cost_estimate=cost(2),
        name="parts",
    )(
        proj_index,
        projectors,
        jnp.sqrt(couplings * (1.0 / HALF)).T,
        potential.reshape(64, LANES),
        meta,
    )
    others = [parts] + [swap(parts, d) for d in range(1, group)]

    field = panel.reshape(bands * 64, LANES)
    size = nb * 64
    forward = []
    for chunk in range(CHUNKS):
        own = [
            lax.dynamic_slice_in_dim(field, (chunk * group + (me ^ d)) * size, size, 0)
            for d in range(group)
        ]
        forward.append([own[0]] + [swap(own[d], d) for d in range(1, group)])

    root_tiles = group * count * 8 // (2 * fold)
    diag, roots, places = pl.pallas_call(
        functools.partial(setup_kernel, gx, gy, nb, count, fold),
        out_shape=[
            shape(rows, SUBS, LANES),
            shape(root_tiles, SUBS, LANES),
            shape(2 * group * count, dtype=jnp.int32),
        ],
        in_specs=[SMEM] + [ANY] * group,
        out_specs=[VMEM, VMEM, SMEM],
        scratch_shapes=[
            pltpu.VMEM((rows * SUBS, LANES), F32),
            pltpu.VMEM((group * 4 * count, LANES), F32),
            pltpu.SMEM((group * 8, LANES), F32),
            pltpu.SemaphoreType.DMA((1,)),
        ],
        cost_estimate=cost(4),
        name="setup",
    )(me_arr, *others)

    weights = jnp.asarray(line_weights())
    summing = np.kron(np.eye(2 * fold), np.ones((TILE // fold, TILE // fold)))
    summing = jnp.asarray(np.concatenate([summing, summing], axis=0).astype(ml_dtypes.bfloat16))
    pair_one = [(s, s ^ 1) for s in range(gz)]
    pair_two = [(s, (s + (1 if s % 2 else -1)) % gz) for s in range(gz)]

    tile_shape = shape(rows * SUBS, LANES)
    edge_shape = shape(pairs, SUBS, LANES)
    states = []
    for chunk in range(CHUNKS):
        tiles, one, two = pl.pallas_call(
            functools.partial(unpack_kernel, gx, gy, nb),
            out_shape=[tile_shape, edge_shape, edge_shape],
            in_specs=[SMEM, SMEM] + [ANY] * group,
            out_specs=[VMEM] * 3,
            scratch_shapes=[
                pltpu.VMEM((rows * SUBS, LANES), F32),
                pltpu.SemaphoreType.DMA((1,)),
            ],
            cost_estimate=cost(3),
            name="unpack",
        )(me_arr, places, *forward[chunk])
        states.append((None, tiles, one, two))

    results = [None] * CHUNKS
    for degree_step in range(DEGREE):
        first, last = degree_step == 0, degree_step == DEGREE - 1
        for chunk in range(CHUNKS):
            prev, tiles, one, two = states[chunk]
            one = lax.ppermute(one, "gz", pair_one)
            two = lax.ppermute(two, "gz", pair_two)
            operands = [me_arr, places, tiles]
            if not first:
                operands.append(prev)
            operands += [diag, roots, one, two, weights, summing]
            scratch = [pltpu.VMEM((rows * SUBS, LANES), F32)]
            if last:
                out_shape = [shape(size, LANES)] * group
                out_specs = [ANY] * group
                scratch += [
                    pltpu.VMEM((rows * SUBS, LANES), F32),
                    pltpu.SemaphoreType.DMA((1,)),
                ]
            else:
                out_shape = [tile_shape, edge_shape, edge_shape]
                out_specs = [VMEM] * 3
            outs = pl.pallas_call(
                functools.partial(step_kernel, gx, gy, nb, count, fold, first, last),
                out_shape=out_shape,
                in_specs=[SMEM, SMEM] + [VMEM] * (len(operands) - 2),
                out_specs=out_specs,
                scratch_shapes=scratch,
                compiler_params=pltpu.CompilerParams(vmem_limit_bytes=24 << 20),
                cost_estimate=cost(5),
                name="step",
            )(*operands)
            if last:
                results[chunk] = [outs[0]] + [swap(outs[d], d) for d in range(1, group)]
            else:
                states[chunk] = (tiles, *outs)

    filtered, gram = pl.pallas_call(
        functools.partial(gather_kernel, group, nb, bands),
        out_shape=[shape(bands * 64, LANES), shape(bands, bands)],
        in_specs=[SMEM] + [ANY] * (CHUNKS * group),
        out_specs=[ANY, VMEM],
        scratch_shapes=[
            pltpu.VMEM((bands * 64, LANES), F32),
            pltpu.SemaphoreType.DMA((1,)),
        ],
        cost_estimate=cost(5),
        name="gather",
    )(me_arr, *[block for chunk in results for block in chunk])

    total_cells = size_x * size_y * size_z * group * gz
    gram = gram * (1.0 / total_cells)
    gram = gram + swap(gram, 1)
    d = 2
    while d < group:
        if 2 * d < group:
            gram = gram + (swap(gram, d) + swap(gram, 2 * d) + swap(gram, 3 * d))
        else:
            gram = gram + swap(gram, d)
        d *= 4
    share = bands // gz
    terms = []
    for d in range(gz):
        term = lax.dynamic_slice_in_dim(gram, (me_z ^ d) * share, share, 0)
        terms.append(swap_z(term, d) if d else term)
    return filtered.reshape(panel.shape), sum(terms[1:], terms[0])


def solution(mesh):
    placed = (
        P(None, "gx", "gy", "gz"),
        P("gx", "gy", "gz"),
        P(("gx", "gy", "gz"), None),
        P(("gx", "gy", "gz"), None),
        P(("gx", "gy", "gz"), None, None),
        P(("gx", "gy", "gz"), None),
    )
    return jax.shard_map(
        shards,
        mesh=mesh,
        in_specs=placed,
        out_specs=(P(None, "gx", "gy", "gz"), P("gz", None)),
        check_vma=False,
    )
```

```python
import functools
import math

import jax
import jax.numpy as jnp
import ml_dtypes
import numpy as np
from jax import lax
from jax.experimental import pallas as pl
from jax.experimental.pallas import tpu as pltpu
from jax.sharding import PartitionSpec as P

DEGREE = 4
CHUNKS = 2

STENCIL = (
    -5369.0 / 1800.0,
    12.0 / 7.0,
    -15.0 / 56.0,
    10.0 / 189.0,
    -1.0 / 112.0,
    2.0 / 1925.0,
    -1.0 / 16632.0,
)
SPACING = 0.224
CENTER = 210.5
HALF = 209.5
REACH = 6
TILE = 64
LANES = 128
SUBS = 8
KINETIC = -0.5 / (SPACING * SPACING) / HALF
TAPS = tuple(KINETIC * c for c in STENCIL)
DIAGONAL = 3.0 * TAPS[0] - CENTER / HALF

F32 = jnp.float32
BF16 = jnp.bfloat16
VMEM = pl.BlockSpec(memory_space=pltpu.VMEM)
SMEM = pl.BlockSpec(memory_space=pltpu.SMEM)
ANY = pl.BlockSpec(memory_space=pl.ANY)
HBM = pl.BlockSpec(memory_space=pltpu.HBM)


PARAMS = pltpu.CompilerParams(vmem_limit_bytes=24 << 20)


def split_halves(matrix):
    high = matrix.astype(ml_dtypes.bfloat16)
    low = (matrix - high.astype(np.float64)).astype(ml_dtypes.bfloat16)
    wide = np.concatenate([high, low], axis=1)
    return np.concatenate([wide, wide], axis=0)


def line_weights():
    own = np.zeros((LANES, LANES))
    halo = np.zeros((8, LANES, LANES))
    for k in range(1, REACH + 1):
        for z in range(LANES):
            for cell in (z + k, z - k):
                if 0 <= cell < LANES:
                    own[cell, z] = TAPS[k]
                else:
                    lane = 8 + cell - LANES if cell >= LANES else 8 + cell
                    for slot in range(8):
                        halo[slot, 16 * slot + lane, z] = TAPS[k]
    return split_halves(own), np.stack([split_halves(slot) for slot in halo])


def halves(value):
    high = value.astype(BF16)
    low = (value - high.astype(F32)).astype(BF16)
    return high, low


def parts_kernel(count, fold, index_ref, proj_ref, root_ref, pot_ref, meta_ref, out_ref):
    out_ref[0:64, :] = pot_ref[...]
    point = lax.broadcasted_iota(jnp.int32, (TILE, TILE), 0)
    width = TILE // fold
    sorted_rows = []
    for atom in range(count):
        order = index_ref[atom : atom + 1, :]
        if fold == 2:
            order = ((order >> 4) & 1) * width + (order >> 5) * 16 + (order & 15)
        hot = (point == order).astype(F32)
        sorted_rows.append(
            lax.dot_general(
                proj_ref[atom],
                hot,
                (((1,), (1,)), ((), ())),
                precision=lax.Precision.HIGHEST,
                preferred_element_type=F32,
            )
            * root_ref[:, atom : atom + 1]
        )
    row = 64
    for first in range(0, count, 2 * fold):
        for f in range(fold):
            out_ref[row : row + 8, :] = jnp.concatenate(
                [sorted_rows[first + q][:, f * width : (f + 1) * width] for q in range(2 * fold)],
                axis=1,
            )
            row += 8
    out_ref[row : row + 8, :] = meta_ref[...]


def swapped(rows):
    if len(rows) == 1:
        return [rows[0][y : y + 1] for y in range(8)]
    return jnp.swapaxes(jnp.stack(rows, axis=0), 0, 1)


def column_sources(me, crossed, beside, size, core):
    pairs = []
    for n, block in enumerate(crossed):
        pairs.append((me ^ (2 * n), block.at[pl.ds(pl.multiple_of(core * size, 8), size)]))
        pairs.append((me ^ (2 * n) ^ 1, beside.at[pl.ds(n * size, size)]))
    return pairs


def setup_kernel(gx, gy, nb, count, fold, me_ref, after_ref, *refs):
    half = gx * gy // 2
    diag_ref, roots_ref, meta_ref, raw, sem = refs[half:]
    rows = 4 * count
    sources = []
    for n in range(half):
        for other in range(2):
            at = 2 * nb * 64 + other * (72 + rows)
            sources.append((me_ref[0] ^ (2 * n + other), refs[n].at[pl.ds(at, 72 + rows)]))
    copies = [
        pltpu.make_async_copy(
            source.at[pl.ds(64 + rows, 8)],
            raw.at[pl.ds(pl.multiple_of(slot * 8, 8), 8)],
            sem.at[0],
        )
        for slot, source in sources
    ]
    for copy in copies:
        copy.start()
    sub = lax.broadcasted_iota(jnp.int32, (SUBS, LANES), 0)
    per_slot = count // (2 * fold)
    for slot, source in sources:
        i, j = slot // gy, slot % gy
        for x in range(8):
            value = source[x * 8 : x * 8 + 8, :] * (1.0 / HALF) + DIAGONAL
            for y in range(8):
                at = ((j * 8 + y) * 8 + x) * SUBS + i * nb
                diag_ref[pl.ds(at, nb)] = jnp.broadcast_to(value[y : y + 1], (nb, LANES))
        for m in range(per_slot):
            for k in range(8):
                parts = []
                for f in range(fold):
                    at = 64 + (m * fold + f) * 8 + k
                    parts.append(jnp.broadcast_to(source[at : at + 1, :], (SUBS, LANES)))
                value = parts[0] if fold == 1 else jnp.where(sub < SUBS // 2, parts[0], parts[1])
                roots_ref[(slot * per_slot + m) * 8 + k] = value
    for copy in copies:
        copy.wait()

    def corners(slot, carry):
        for atom in range(count):
            n = slot * count + atom
            first = (raw[slot * 8, atom].astype(jnp.int32) + (slot % gy) * 64) * SUBS
            meta_ref[2 * n] = first + (slot // gy * nb if fold == 2 else 0)
            meta_ref[2 * n + 1] = raw[slot * 8, count + atom].astype(jnp.int32)
        return carry

    lax.fori_loop(0, gx * gy, corners, 0)


def pack_edges(values, lane):
    wide = []
    for first in (0, 8):
        tile = None
        for slot in range(8):
            moved = pltpu.roll(values[first + slot], (16 * slot + 2 + REACH) % LANES, 1)
            tile = moved if tile is None else jnp.where((lane >> 4) == slot, moved, tile)
        wide.append(tile)
    lower = (lane & 15) < 8
    low = jnp.where(lower, pltpu.roll(wide[0], LANES - 8, 1), wide[1])
    high = jnp.where(lower, wide[0], pltpu.roll(wide[1], 8, 1))
    return low, high


def send_edges(even, low, high):
    return jnp.where(even, high, low), jnp.where(even, low, high)


def pack_kernel(group, size, chunk, tables, me_ref, field, passed, *refs):
    blocks, sem = refs[2 if tables else 1 : -1], refs[-1]
    copies = []
    for n, block in enumerate(blocks):
        chip = me_ref[0] // 2 ^ n
        row = (chunk * group + chip * 2 + me_ref[0] % 2) * size
        copies.append(
            pltpu.make_async_copy(
                field.at[pl.ds(pl.multiple_of(row, 64), size)],
                block.at[pl.ds(0, size)],
                sem.at[0],
            )
        )
    for copy in copies:
        copy.start()
    for n, block in enumerate(blocks):
        chip = me_ref[0] // 2 ^ n
        block[pl.ds(size, size)] = passed[pl.ds(pl.multiple_of(chip * size, 64), size)]
        if tables:
            block[pl.ds(2 * size, tables)] = refs[0][...]
            block[pl.ds(2 * size + tables, tables)] = refs[1][...]
    for copy in copies:
        copy.wait()


def unpack_kernel(gx, gy, nb, me_ref, after_ref, *refs):
    half = gx * gy // 2
    z_ref, one_ref, two_ref = refs[half:]
    size = nb * 64
    for n in range(half):
        for other in range(2):
            slot = me_ref[0] ^ (2 * n + other)
            i, j = slot // gy, slot % gy
            for x in range(8):
                first = other * size + x * 8
                turned = swapped([refs[n][first + b * 64 : first + b * 64 + 8] for b in range(nb)])
                for y in range(8):
                    z_ref[pl.ds(((j * 8 + y) * 8 + x) * SUBS + i * nb, nb)] = turned[y]
    lane = lax.broadcasted_iota(jnp.int32, (SUBS, LANES), 1)
    even = me_ref[1] == 0

    def lines(pair, carry):
        tiles = z_ref[pl.ds(pl.multiple_of(pair * LANES, LANES), LANES)]
        values = [tiles[SUBS * q : SUBS * (q + 1)] for q in range(16)]
        low, high = pack_edges(values, lane)
        one_ref[pair], two_ref[pair] = send_edges(even, low, high)
        return carry

    lax.fori_loop(0, gy * 4, lines, 0, unroll=4)


def tile_rows(row):
    return pl.ds(pl.multiple_of(row * SUBS, SUBS), SUBS)


def inner_kernel(gx, gy, nb, count, fold, first, after_ref, meta_ref, *refs):
    if first:
        z_ref, diag_ref, roots_ref, w_ref, sum_ref = refs[:5]
    else:
        z_ref, prev_ref, diag_ref, roots_ref, w_ref, sum_ref = refs[:6]
    out_ref, atoms_ref, acc, tile_ref, spread_ref = refs[-5:]
    group = gx * gy
    ny = gy * 8
    width = TILE // fold
    per_tile = 2 * fold
    per_slot = count // per_tile
    lane = lax.broadcasted_iota(jnp.int32, (SUBS, LANES), 1)
    sub = lax.broadcasted_iota(jnp.int32, (SUBS, LANES), 0)

    def tile_row(t):
        return ((t % 4) * 8 + (t // 4) * fold) * SUBS

    def gather(slot):
        for m in range(per_slot):
            tile = jnp.zeros((SUBS, LANES), F32)
            for q in range(per_tile):
                n = slot * count + per_tile * m + q
                start = meta_ref[2 * n]
                back = LANES - meta_ref[2 * n + 1]
                for t in range(16 // fold):
                    value = z_ref[pl.ds(start + tile_row(t), SUBS)]
                    if fold == 2:
                        beyond = z_ref[pl.ds(start + (tile_row(t) + nb), SUBS)]
                        value = jnp.where(sub < nb, value, beyond)
                    value = pltpu.roll(value, back + (4 * t + width * q), 1)
                    tile = jnp.where((lane >> 2) == t + q * (width // 4), value, tile)
            tile_ref[slot * per_slot + m] = tile

    def scatter(slot, i):
        for m in range(per_slot):
            spread = spread_ref[slot * per_slot + m]
            for q in range(per_tile):
                n = slot * count + per_tile * m + q
                start = meta_ref[2 * n]
                z0 = meta_ref[2 * n + 1]
                inside = (lane >= z0) & (lane < z0 + 4)
                if fold == 1:
                    masks = [inside & (sub // nb == i)]
                else:
                    masks = [inside & (sub < nb), inside & (sub >= nb)]
                sums = []
                for t in range(16 // fold):
                    value = pltpu.roll(spread, z0 + (LANES - 4 * t - width * q), 1)
                    for f, mask in enumerate(masks):
                        here = pl.ds(start + (tile_row(t) + f * nb), SUBS)
                        sums.append((here, atoms_ref[here] + jnp.where(mask, value, 0.0)))
                for here, value in sums:
                    atoms_ref[here] = value

    def second_dim(x, carry):
        for c in range(group // 8):
            gather(x * (group // 8) + c)
        block = pl.ds(pl.multiple_of(x * 32 * SUBS, 32 * SUBS), 32 * SUBS)
        operand = jnp.concatenate(halves(z_ref[block]), axis=1)
        product = jnp.dot(operand, w_ref[...], preferred_element_type=F32)
        out_ref[block] = product[:, :LANES] + product[:, LANES:]
        values = [z_ref[tile_rows(y * 8 + x)] for y in range(ny)]
        for y in range(ny):
            total = None
            for k in range(1, REACH + 1):
                term = TAPS[k] * (values[(y + k) % ny] + values[(y - k) % ny])
                total = term if total is None else total + term
            acc[tile_rows(y * 8 + x)] = total
            atoms_ref[tile_rows(y * 8 + x)] = jnp.zeros((SUBS, LANES), F32)
        return carry

    lax.fori_loop(0, 8, second_dim, 0, unroll=2)

    def contract(eight, carry):
        products = []
        for m in range(8):
            tile = tile_ref[eight * 8 + m]
            for k in range(8):
                products.append(tile * roots_ref[(eight * 8 + m) * 8 + k])
        sums = jnp.dot(
            jnp.concatenate(halves(jnp.concatenate(products, axis=0)), axis=1),
            sum_ref[...],
            preferred_element_type=F32,
        )
        for m in range(8):
            spread = None
            for k in range(8):
                at = (m * 8 + k) * SUBS
                coeff = sums[at : at + SUBS]
                if fold == 2:
                    coeff = coeff + pltpu.roll(coeff, nb, 0)
                term = coeff * roots_ref[(eight * 8 + m) * 8 + k]
                spread = term if spread is None else spread + term
            spread_ref[eight * 8 + m] = spread if first else 2.0 * spread
        return carry

    lax.fori_loop(0, group * per_slot // 8, contract, 0, unroll=2)

    def rest(four):
        for q in range(4):
            values = [z_ref[tile_rows(four * 32 + 8 * q + x)] for x in range(8)]
            after = [pltpu.roll(value, SUBS - nb, 0) for value in values]
            before = after if gx == 2 else [pltpu.roll(value, nb, 0) for value in values]
            wide = before + values + after
            for x in range(8):
                here = tile_rows(four * 32 + 8 * q + x)
                total = acc[here] + out_ref[here]
                total = total + diag_ref[here] * values[x]
                for k in range(1, REACH + 1):
                    total = total + TAPS[k] * (wide[8 + x + k] + wide[8 + x - k])
                if not first:
                    total = 2.0 * total - prev_ref[here]
                out_ref[here] = total

    def block(j, carry):
        for half in range(2):
            for i in range(half * gx // 2, (half + 1) * gx // 2):
                scatter(i * gy + j, i)
            rest(2 * j + half)
        return carry

    lax.fori_loop(0, gy, block, 0)


def outer_kernel(gx, gy, nb, first, last, edge, me_ref, part_ref, atoms_ref, one_in, two_in, *refs):
    group = gx * gy
    w_ref, refs = refs[0], refs[1:]
    if last:
        blocks, acc = refs[: group // 2], refs[group // 2]
    else:
        acc, one_ref, two_ref = refs
    lane = lax.broadcasted_iota(jnp.int32, (SUBS, LANES), 1)
    even = me_ref[1] == 0
    lower = (lane & 15) < 8
    ny = gy * 8
    tiles = []
    for pair in range(ny // 2):
        one = one_in[edge + pair]
        two = two_in[edge + pair]
        below = jnp.where(even, two, one)
        above = jnp.where(even, one, two)
        tiles.append(jnp.where(lower, below, pltpu.roll(above, 8, 1)))
        tiles.append(jnp.where(lower, pltpu.roll(below, LANES - 8, 1), above))
    halo = jnp.concatenate(tiles, axis=0)
    operand = jnp.concatenate(halves(halo if first else 2.0 * halo), axis=1)
    for x in range(8):
        product = jnp.dot(operand, w_ref[x], preferred_element_type=F32)
        third = product[:, :LANES] + product[:, LANES:]
        for y in range(ny):
            here = pl.ds((y * 8 + x) * SUBS, SUBS)
            acc[here] = part_ref[here] + atoms_ref[here] + third[y * SUBS : (y + 1) * SUBS]
    if not last:

        def edges(pair, carry):
            rows = acc[pl.ds(pl.multiple_of(pair * LANES, LANES), LANES)]
            low, high = pack_edges([rows[SUBS * m : SUBS * (m + 1)] for m in range(16)], lane)
            one_ref[pair], two_ref[pair] = send_edges(even, low, high)
            return carry

        lax.fori_loop(0, ny // 2, edges, 0, unroll=4)
    if last:
        size = nb * 64
        for n in range(group // 2):
            for core in range(2):
                slot = (me_ref[0] // 2 ^ n) * 2 + core
                i, j = slot // gy, slot % gy
                for x in range(8):
                    rows = [
                        acc[pl.ds(((j * 8 + y) * 8 + x) * SUBS + i * nb, nb)] for y in range(8)
                    ]
                    if nb == 1:
                        turned = [jnp.concatenate(rows, axis=0)]
                    else:
                        turned = jnp.swapaxes(jnp.stack(rows, axis=0), 0, 1)
                    for b in range(nb):
                        at = core * size + b * 64 + x * 8
                        blocks[n][at : at + 8] = turned[b]


def turn(ref, first):
    return swapped(
        [ref[pl.ds(pl.multiple_of(first + 64 * s, SUBS), SUBS)] for s in range(SUBS)]
    )


def gather_kernel(group, nb, bands, scale, me_ref, *refs):
    half = group // 2
    out_ref, gram_ref, field, sem = refs[CHUNKS * (half + 1) :]
    size = nb * 64
    for chunk in range(CHUNKS):
        blocks = refs[chunk * (half + 1) : (chunk + 1) * (half + 1)]
        for slot, source in column_sources(
            me_ref[0], blocks[:half], blocks[half], size, me_ref[0] % 2
        ):
            row = (chunk * group + slot) * size
            field[pl.ds(pl.multiple_of(row, 64), size)] = source[...]
    store = pltpu.make_async_copy(field, out_ref, sem.at[0])
    store.start()
    gram_ref[...] = jnp.zeros_like(gram_ref)

    def cells(n, carry):
        total = None
        turned = [turn(field, g * SUBS * 64 + n * 8) for g in range(bands // SUBS)]
        for m in range(4):
            pieces = []
            for c in range(2):
                cell = m * 2 + c
                pieces.append(jnp.concatenate([group_[cell] for group_ in turned], axis=0))
            value = jnp.concatenate(pieces, axis=1)
            high, low = halves(value)
            both = jnp.concatenate([high, low], axis=0)
            product = lax.dot_general(
                both, both, (((1,), (1,)), ((), ())), preferred_element_type=F32
            )
            total = product if total is None else total + product
        gram_ref[...] += (
            total[:bands, :bands]
            + total[bands:, :bands]
            + total[:bands, bands:]
            + total[bands:, bands:]
        )
        return carry

    lax.fori_loop(0, 8, cells, 0)
    gram_ref[...] *= scale
    store.wait()


def shape(*dims, dtype=F32):
    return jax.ShapeDtypeStruct(dims, dtype)


def cost(microseconds):
    return pl.CostEstimate(
        flops=int(microseconds * 1e9), bytes_accessed=int(microseconds * 3e6), transcendentals=0
    )


def shards(panel, potential, atom_corner, proj_index, projectors, couplings):
    bands, size_x, size_y, size_z = panel.shape
    count, nproj = couplings.shape
    gx, gy, gz = lax.axis_size("gx"), lax.axis_size("gy"), lax.axis_size("gz")
    group = gx * gy
    nb = bands // (CHUNKS * group)
    fold = 2 if gx == 2 else 1
    column = ("gx", "gy")
    me = lax.axis_index("gx") * gy + lax.axis_index("gy")
    me_z = lax.axis_index("gz")
    me_arr = jnp.stack([me, me_z % 2])
    rows = gy * 64
    pairs = gy * 4

    def swap(block, d):
        return lax.ppermute(block, column, [(s, s ^ d) for s in range(group)])

    def swap_z(block, d):
        return lax.ppermute(block, "gz", [(s, s ^ d) for s in range(gz)])

    anchor = jnp.stack(
        [
            lax.axis_index("gx") * size_x,
            lax.axis_index("gy") * size_y,
            me_z * size_z,
        ]
    )
    local = atom_corner - anchor[None, :]
    meta = jnp.concatenate([local[:, 1] * 8 + local[:, 0], local[:, 2]]).astype(F32)
    meta = jnp.broadcast_to(jnp.pad(meta, (0, LANES - 2 * count))[None], (8, LANES))
    part_rows = 64 + 4 * count + 8
    size = nb * 64
    core = me % 2

    def cross(blocks):
        return [blocks[0]] + [swap(blocks[n], 2 * n) for n in range(1, group // 2)]

    def beside(crossed):
        halves_of = [lax.dynamic_slice_in_dim(b, (1 - core) * size, size, 0) for b in crossed]
        return swap(jnp.concatenate(halves_of, axis=0), 1)

    field = panel.reshape(bands * 64, LANES)
    parts = pl.pallas_call(
        functools.partial(parts_kernel, count, fold),
        out_shape=shape(part_rows, LANES),
        in_specs=[VMEM] * 5,
        out_specs=VMEM,
        compiler_params=PARAMS,
        cost_estimate=cost(1),
        name="parts",
    )(
        proj_index,
        projectors,
        jnp.sqrt(couplings * (1.0 / HALF)).T,
        potential.reshape(64, LANES),
        meta,
    )
    packed = []
    forward = []
    for chunk in range(CHUNKS):
        tables = part_rows if chunk == 0 else 0
        mine = lax.dynamic_slice_in_dim(field, chunk * group * size, group * size, 0)
        mine = mine.reshape(group // 2, 2, size, LANES)
        passed = lax.dynamic_slice_in_dim(mine, 1 - core, 1, 1).reshape(group // 2 * size, LANES)
        passed = swap(passed, 1)
        if chunk == 0:
            extra = [parts, swap(parts, 1)]
            field, passed = lax.optimization_barrier((field, passed))
        else:
            extra = packed[0][:1]
        packed.append(
            pl.pallas_call(
                functools.partial(pack_kernel, group, size, chunk, tables),
                out_shape=[shape(2 * (size + tables), LANES)] * (group // 2),
                in_specs=[SMEM, HBM, VMEM] + ([ANY] if chunk else [VMEM] * 2),
                out_specs=[VMEM] * (group // 2),
                scratch_shapes=[pltpu.SemaphoreType.DMA((1,))],
                compiler_params=PARAMS,
                cost_estimate=cost(1),
                name="pack",
            )(me_arr, field, passed, *extra)
        )
        forward.append(cross(packed[chunk]))

    tile_shape = shape(rows * SUBS, LANES)
    edge_shape = shape(pairs, SUBS, LANES)
    def unpack(chunk, after):
        tiles, one, two = pl.pallas_call(
            functools.partial(unpack_kernel, gx, gy, nb),
            out_shape=[tile_shape, edge_shape, edge_shape],
            in_specs=[SMEM, ANY] + [VMEM] * (group // 2),
            out_specs=[VMEM] * 3,
            compiler_params=PARAMS,
            cost_estimate=cost(2),
            name="unpack",
        )(me_arr, after, *forward[chunk])
        return None, tiles, one, two

    states = [unpack(0, packed[-1][0])]
    root_tiles = group * count * 8 // (2 * fold)
    diag, roots, places = pl.pallas_call(
        functools.partial(setup_kernel, gx, gy, nb, count, fold),
        out_shape=[
            shape(rows * SUBS, LANES),
            shape(root_tiles, SUBS, LANES),
            shape(2 * group * count, dtype=jnp.int32),
        ],
        in_specs=[SMEM, ANY] + [VMEM] * (group // 2),
        out_specs=[VMEM, VMEM, SMEM],
        scratch_shapes=[
            pltpu.SMEM((group * 8, LANES), F32),
            pltpu.SemaphoreType.DMA((1,)),
        ],
        compiler_params=PARAMS,
        cost_estimate=cost(2),
        name="setup",
    )(me_arr, states[0][2], *forward[0])
    for chunk in range(1, CHUNKS):
        states.append(unpack(chunk, roots))

    own_weights, halo_weights = (jnp.asarray(w) for w in line_weights())
    summing = np.kron(np.eye(2 * fold), np.ones((TILE // fold, TILE // fold)))
    summing = jnp.asarray(np.concatenate([summing, summing], axis=0).astype(ml_dtypes.bfloat16))
    pair_one = [(s, s ^ 1) for s in range(gz)]
    pair_two = [(s, (s + (1 if s % 2 else -1)) % gz) for s in range(gz)]

    results = [None] * CHUNKS
    for degree_step in range(DEGREE):
        first, last = degree_step == 0, degree_step == DEGREE - 1
        outs = None
        if not first:
            joint_one = jnp.concatenate([state[2] for state in states], axis=0)
            joint_two = jnp.concatenate([state[3] for state in states], axis=0)
            joint_one = lax.ppermute(joint_one, "gz", pair_one)
            joint_two = lax.ppermute(joint_two, "gz", pair_two)
        for chunk in range(CHUNKS):
            prev, tiles, one, two = states[chunk]
            edge = 0 if first else chunk * pairs
            if first:
                one = lax.ppermute(one, "gz", pair_one)
                two = lax.ppermute(two, "gz", pair_two)
            else:
                one, two = joint_one, joint_two
            after = roots if outs is None or not last else outs[0]
            operands = [after, places, tiles]
            if not first:
                operands.append(prev)
            operands += [diag, roots, own_weights, summing]
            part, atoms = pl.pallas_call(
                functools.partial(inner_kernel, gx, gy, nb, count, fold, first),
                out_shape=[tile_shape, tile_shape],
                in_specs=[ANY, SMEM] + [VMEM] * (len(operands) - 2),
                out_specs=[VMEM] * 2,
                scratch_shapes=[pltpu.VMEM((rows * SUBS, LANES), F32)]
                + [pltpu.VMEM((root_tiles // 8, SUBS, LANES), F32)] * 2,
                compiler_params=PARAMS,
                cost_estimate=cost(4),
                name="inner",
            )(*operands)
            outs = pl.pallas_call(
                functools.partial(outer_kernel, gx, gy, nb, first, last, edge),
                out_shape=[shape(2 * size, LANES)] * (group // 2)
                if last
                else [tile_shape, edge_shape, edge_shape],
                in_specs=[SMEM] + [VMEM] * 5,
                out_specs=[VMEM] * (group // 2 if last else 3),
                scratch_shapes=[pltpu.VMEM((rows * SUBS, LANES), F32)] * last,
                compiler_params=PARAMS,
                cost_estimate=cost(1),
                name="outer",
            )(me_arr, part, atoms, one, two, halo_weights)
            if last:
                crossed = cross(outs)
                results[chunk] = crossed + [beside(crossed)]
            else:
                states[chunk] = (tiles, *outs)

    total_cells = size_x * size_y * size_z * group * gz
    filtered, gram = pl.pallas_call(
        functools.partial(gather_kernel, group, nb, bands, 1.0 / total_cells),
        out_shape=[shape(bands * 64, LANES), shape(bands, bands)],
        in_specs=[SMEM] + [VMEM] * (CHUNKS * (group // 2 + 1)),
        out_specs=[ANY, VMEM],
        scratch_shapes=[
            pltpu.VMEM((bands * 64, LANES), F32),
            pltpu.SemaphoreType.DMA((1,)),
        ],
        compiler_params=PARAMS,
        cost_estimate=cost(5),
        name="gather",
    )(me_arr, *[block for chunk in results for block in chunk])

    gram = gram + swap(gram, 1)
    d = 2
    while d < group:
        if 2 * d < group:
            gram = gram + (swap(gram, d) + swap(gram, 2 * d) + swap(gram, 3 * d))
        else:
            gram = gram + swap(gram, d)
        d *= 4
    share = bands // gz
    terms = []
    for d in range(gz):
        term = lax.dynamic_slice_in_dim(gram, (me_z ^ d) * share, share, 0)
        terms.append(swap_z(term, d) if d else term)
    return filtered.reshape(panel.shape), sum(terms[1:], terms[0])


def solution(mesh):
    placed = (
        P(None, "gx", "gy", "gz"),
        P("gx", "gy", "gz"),
        P(("gx", "gy", "gz"), None),
        P(("gx", "gy", "gz"), None),
        P(("gx", "gy", "gz"), None, None),
        P(("gx", "gy", "gz"), None),
    )
    return jax.shard_map(
        shards,
        mesh=mesh,
        in_specs=placed,
        out_specs=(P(None, "gx", "gy", "gz"), P("gz", None)),
        check_vma=False,
    )
```

```python
import functools
import math

import jax
import jax.numpy as jnp
import ml_dtypes
import numpy as np
from jax import lax
from jax.experimental import pallas as pl
from jax.experimental.pallas import tpu as pltpu
from jax.sharding import PartitionSpec as P

DEGREE = 4
CHUNKS = 2

STENCIL = (
    -5369.0 / 1800.0,
    12.0 / 7.0,
    -15.0 / 56.0,
    10.0 / 189.0,
    -1.0 / 112.0,
    2.0 / 1925.0,
    -1.0 / 16632.0,
)
SPACING = 0.224
CENTER = 210.5
HALF = 209.5
REACH = 6
TILE = 64
LANES = 128
SUBS = 8
KINETIC = -0.5 / (SPACING * SPACING) / HALF
TAPS = tuple(KINETIC * c for c in STENCIL)
DIAGONAL = 3.0 * TAPS[0] - CENTER / HALF

F32 = jnp.float32
BF16 = jnp.bfloat16
VMEM = pl.BlockSpec(memory_space=pltpu.VMEM)
SMEM = pl.BlockSpec(memory_space=pltpu.SMEM)
ANY = pl.BlockSpec(memory_space=pl.ANY)
HBM = pl.BlockSpec(memory_space=pltpu.HBM)


PARAMS = pltpu.CompilerParams(vmem_limit_bytes=24 << 20)


def split_halves(matrix):
    high = matrix.astype(ml_dtypes.bfloat16)
    low = (matrix - high.astype(np.float64)).astype(ml_dtypes.bfloat16)
    wide = np.concatenate([high, low], axis=1)
    return np.concatenate([wide, wide], axis=0)


def line_weights():
    own = np.zeros((LANES, LANES))
    halo = np.zeros((8, LANES, LANES))
    for k in range(1, REACH + 1):
        for z in range(LANES):
            for cell in (z + k, z - k):
                if 0 <= cell < LANES:
                    own[cell, z] = TAPS[k]
                else:
                    lane = 8 + cell - LANES if cell >= LANES else 8 + cell
                    for slot in range(8):
                        halo[slot, 16 * slot + lane, z] = TAPS[k]
    return split_halves(own), np.stack([split_halves(slot) for slot in halo])


def halves(value):
    high = value.astype(BF16)
    low = (value - high.astype(F32)).astype(BF16)
    return high, low


def parts_kernel(count, fold, index_ref, proj_ref, root_ref, pot_ref, meta_ref, out_ref):
    out_ref[0:64, :] = pot_ref[...]
    point = lax.broadcasted_iota(jnp.int32, (TILE, TILE), 0)
    width = TILE // fold
    sorted_rows = []
    for atom in range(count):
        order = index_ref[atom : atom + 1, :]
        if fold == 2:
            order = ((order >> 4) & 1) * width + (order >> 5) * 16 + (order & 15)
        hot = (point == order).astype(F32)
        sorted_rows.append(
            lax.dot_general(
                proj_ref[atom],
                hot,
                (((1,), (1,)), ((), ())),
                precision=lax.Precision.HIGHEST,
                preferred_element_type=F32,
            )
            * root_ref[:, atom : atom + 1]
        )
    row = 64
    for first in range(0, count, 2 * fold):
        for f in range(fold):
            out_ref[row : row + 8, :] = jnp.concatenate(
                [sorted_rows[first + q][:, f * width : (f + 1) * width] for q in range(2 * fold)],
                axis=1,
            )
            row += 8
    out_ref[row : row + 8, :] = meta_ref[...]


def swapped(rows):
    if len(rows) == 1:
        return [rows[0][y : y + 1] for y in range(8)]
    return jnp.swapaxes(jnp.stack(rows, axis=0), 0, 1)


def column_sources(me, crossed, beside, size, core):
    pairs = []
    for n, block in enumerate(crossed):
        pairs.append((me ^ (2 * n), block.at[pl.ds(pl.multiple_of(core * size, 8), size)]))
        pairs.append((me ^ (2 * n) ^ 1, beside.at[pl.ds(n * size, size)]))
    return pairs


def atoms_kernel(gx, gy, nb, count, fold, me_ref, after_ref, *refs):
    half = gx * gy // 2
    roots_ref, meta_ref, raw, sem = refs[half:]
    rows = 4 * count + 8
    sources = []
    for n in range(half):
        for other in range(2):
            at = 2 * nb * 64 + other * rows
            sources.append((me_ref[0] ^ (2 * n + other), refs[n].at[pl.ds(at, rows)]))
    copies = [
        pltpu.make_async_copy(
            source.at[pl.ds(rows - 8, 8)],
            raw.at[pl.ds(pl.multiple_of(slot * 8, 8), 8)],
            sem.at[0],
        )
        for slot, source in sources
    ]
    for copy in copies:
        copy.start()
    sub = lax.broadcasted_iota(jnp.int32, (SUBS, LANES), 0)
    per_slot = count // (2 * fold)
    for slot, source in sources:
        for m in range(per_slot):
            for k in range(8):
                parts = []
                for f in range(fold):
                    at = (m * fold + f) * 8 + k
                    parts.append(jnp.broadcast_to(source[at : at + 1, :], (SUBS, LANES)))
                value = parts[0] if fold == 1 else jnp.where(sub < SUBS // 2, parts[0], parts[1])
                roots_ref[(slot * per_slot + m) * 8 + k] = value
    for copy in copies:
        copy.wait()

    def corners(slot, carry):
        for atom in range(count):
            n = slot * count + atom
            first = (raw[slot * 8, atom].astype(jnp.int32) + (slot % gy) * 64) * SUBS
            meta_ref[2 * n] = first + (slot // gy * nb if fold == 2 else 0)
            meta_ref[2 * n + 1] = raw[slot * 8, count + atom].astype(jnp.int32)
        return carry

    lax.fori_loop(0, gx * gy, corners, 0)


def diagonal_kernel(gx, gy, nb, me_ref, after_ref, *refs):
    half = gx * gy // 2
    diag_ref = refs[half]
    for n in range(half):
        for other in range(2):
            slot = me_ref[0] ^ (2 * n + other)
            i, j = slot // gy, slot % gy
            for x in range(8):
                first = 2 * nb * 64 + other * 64 + x * 8
                value = refs[n][first : first + 8, :] * (1.0 / HALF) + DIAGONAL
                for y in range(8):
                    at = ((j * 8 + y) * 8 + x) * SUBS + i * nb
                    diag_ref[pl.ds(at, nb)] = jnp.broadcast_to(value[y : y + 1], (nb, LANES))


def pack_edges(values, lane):
    wide = []
    for first in (0, 8):
        tile = None
        for slot in range(8):
            moved = pltpu.roll(values[first + slot], (16 * slot + 2 + REACH) % LANES, 1)
            tile = moved if tile is None else jnp.where((lane >> 4) == slot, moved, tile)
        wide.append(tile)
    lower = (lane & 15) < 8
    low = jnp.where(lower, pltpu.roll(wide[0], LANES - 8, 1), wide[1])
    high = jnp.where(lower, wide[0], pltpu.roll(wide[1], 8, 1))
    return low, high


def send_edges(even, low, high):
    return jnp.where(even, high, low), jnp.where(even, low, high)


def join_kernel(
    group, size, chunk, extra, me_ref, field, after_ref, passed, own_ref, other_ref, *refs
):
    blocks, sem = refs[:-1], refs[-1]
    copies = []
    for n, block in enumerate(blocks):
        chip = me_ref[0] // 2 ^ n
        row = (chunk * group + chip * 2 + me_ref[0] % 2) * size
        copies.append(
            pltpu.make_async_copy(
                field.at[pl.ds(pl.multiple_of(row, 64), size)],
                block.at[pl.ds(0, size)],
                sem.at[0],
            )
        )
    for copy in copies:
        copy.start()
    first, rows = extra
    for n, block in enumerate(blocks):
        chip = me_ref[0] // 2 ^ n
        row = (chunk * group // 2 + chip) * size
        block[pl.ds(size, size)] = passed[pl.ds(pl.multiple_of(row, 64), size)]
        if rows:
            block[pl.ds(2 * size, rows)] = own_ref[pl.ds(first, rows)]
            block[pl.ds(2 * size + rows, rows)] = other_ref[pl.ds(first, rows)]
    for copy in copies:
        copy.wait()


def unpack_kernel(gx, gy, nb, me_ref, after_ref, *refs):
    half = gx * gy // 2
    size = nb * 64
    z_ref, one_ref, two_ref = refs[-3:]
    for n in range(half):
        for other in range(2):
            slot = me_ref[0] ^ (2 * n + other)
            i, j = slot // gy, slot % gy
            for x in range(8):
                first = x * 8 + other * size
                turned = swapped([refs[n][first + b * 64 : first + b * 64 + 8] for b in range(nb)])
                for y in range(8):
                    z_ref[pl.ds(((j * 8 + y) * 8 + x) * SUBS + i * nb, nb)] = turned[y]
    lane = lax.broadcasted_iota(jnp.int32, (SUBS, LANES), 1)
    even = me_ref[1] == 0

    def lines(pair, carry):
        tiles = z_ref[pl.ds(pl.multiple_of(pair * LANES, LANES), LANES)]
        values = [tiles[SUBS * q : SUBS * (q + 1)] for q in range(16)]
        low, high = pack_edges(values, lane)
        one_ref[pair], two_ref[pair] = send_edges(even, low, high)
        return carry

    lax.fori_loop(0, gy * 4, lines, 0, unroll=4)


def tile_rows(row):
    return pl.ds(pl.multiple_of(row * SUBS, SUBS), SUBS)


def inner_kernel(gx, gy, nb, count, fold, first, after_ref, meta_ref, *refs):
    if first:
        z_ref, roots_ref, w_ref, sum_ref = refs[:4]
    else:
        z_ref, prev_ref, diag_ref, roots_ref, w_ref, sum_ref = refs[:6]
    out_ref, atoms_ref, acc, tile_ref, spread_ref = refs[-5:]
    group = gx * gy
    ny = gy * 8
    width = TILE // fold
    per_tile = 2 * fold
    per_slot = count // per_tile
    lane = lax.broadcasted_iota(jnp.int32, (SUBS, LANES), 1)
    sub = lax.broadcasted_iota(jnp.int32, (SUBS, LANES), 0)

    def tile_row(t):
        return ((t % 4) * 8 + (t // 4) * fold) * SUBS

    def gather(slot):
        for m in range(per_slot):
            tile = jnp.zeros((SUBS, LANES), F32)
            for q in range(per_tile):
                n = slot * count + per_tile * m + q
                start = meta_ref[2 * n]
                back = LANES - meta_ref[2 * n + 1]
                for t in range(16 // fold):
                    value = z_ref[pl.ds(start + tile_row(t), SUBS)]
                    if fold == 2:
                        beyond = z_ref[pl.ds(start + (tile_row(t) + nb), SUBS)]
                        value = jnp.where(sub < nb, value, beyond)
                    value = pltpu.roll(value, back + (4 * t + width * q), 1)
                    tile = jnp.where((lane >> 2) == t + q * (width // 4), value, tile)
            tile_ref[slot * per_slot + m] = tile

    def scatter(slot, i):
        for m in range(per_slot):
            spread = spread_ref[slot * per_slot + m]
            for q in range(per_tile):
                n = slot * count + per_tile * m + q
                start = meta_ref[2 * n]
                z0 = meta_ref[2 * n + 1]
                inside = (lane >= z0) & (lane < z0 + 4)
                if fold == 1:
                    masks = [inside & (sub // nb == i)]
                else:
                    masks = [inside & (sub < nb), inside & (sub >= nb)]
                sums = []
                for t in range(16 // fold):
                    value = pltpu.roll(spread, z0 + (LANES - 4 * t - width * q), 1)
                    for f, mask in enumerate(masks):
                        here = pl.ds(start + (tile_row(t) + f * nb), SUBS)
                        sums.append((here, atoms_ref[here] + jnp.where(mask, value, 0.0)))
                for here, value in sums:
                    atoms_ref[here] = value

    def second_dim(x, carry):
        for c in range(group // 8):
            gather(x * (group // 8) + c)
        block = pl.ds(pl.multiple_of(x * 32 * SUBS, 32 * SUBS), 32 * SUBS)
        operand = jnp.concatenate(halves(z_ref[block]), axis=1)
        product = jnp.dot(operand, w_ref[...], preferred_element_type=F32)
        out_ref[block] = product[:, :LANES] + product[:, LANES:]
        values = [z_ref[tile_rows(y * 8 + x)] for y in range(ny)]
        for y in range(ny):
            total = None
            for k in range(1, REACH + 1):
                term = TAPS[k] * (values[(y + k) % ny] + values[(y - k) % ny])
                total = term if total is None else total + term
            acc[tile_rows(y * 8 + x)] = total
            atoms_ref[tile_rows(y * 8 + x)] = jnp.zeros((SUBS, LANES), F32)
        return carry

    lax.fori_loop(0, 8, second_dim, 0, unroll=2)

    def contract(eight, carry):
        products = []
        for m in range(8):
            tile = tile_ref[eight * 8 + m]
            for k in range(8):
                products.append(tile * roots_ref[(eight * 8 + m) * 8 + k])
        sums = jnp.dot(
            jnp.concatenate(halves(jnp.concatenate(products, axis=0)), axis=1),
            sum_ref[...],
            preferred_element_type=F32,
        )
        for m in range(8):
            spread = None
            for k in range(8):
                at = (m * 8 + k) * SUBS
                coeff = sums[at : at + SUBS]
                if fold == 2:
                    coeff = coeff + pltpu.roll(coeff, nb, 0)
                term = coeff * roots_ref[(eight * 8 + m) * 8 + k]
                spread = term if spread is None else spread + term
            spread_ref[eight * 8 + m] = spread if first else 2.0 * spread
        return carry

    lax.fori_loop(0, group * per_slot // 8, contract, 0, unroll=2)

    def rest(four):
        for q in range(4):
            values = [z_ref[tile_rows(four * 32 + 8 * q + x)] for x in range(8)]
            after = [pltpu.roll(value, SUBS - nb, 0) for value in values]
            before = after if gx == 2 else [pltpu.roll(value, nb, 0) for value in values]
            wide = before + values + after
            for x in range(8):
                here = tile_rows(four * 32 + 8 * q + x)
                total = acc[here] + out_ref[here]
                if not first:
                    total = total + diag_ref[here] * values[x]
                for k in range(1, REACH + 1):
                    total = total + TAPS[k] * (wide[8 + x + k] + wide[8 + x - k])
                if not first:
                    total = 2.0 * total - prev_ref[here]
                out_ref[here] = total

    def block(j, carry):
        for half in range(2):
            for i in range(half * gx // 2, (half + 1) * gx // 2):
                scatter(i * gy + j, i)
            rest(2 * j + half)
        return carry

    lax.fori_loop(0, gy, block, 0)


def outer_kernel(
    gx, gy, nb, first, last, edge, me_ref, after_ref, part_ref, atoms_ref, one_in, two_in, w_ref, *refs
):
    group = gx * gy
    if first:
        z_ref, diag_ref, refs = refs[0], refs[1], refs[2:]
    if last:
        blocks, acc = refs[: group // 2], refs[group // 2]
    else:
        acc, one_ref, two_ref = refs
    lane = lax.broadcasted_iota(jnp.int32, (SUBS, LANES), 1)
    even = me_ref[1] == 0
    lower = (lane & 15) < 8
    ny = gy * 8
    tiles = []
    for pair in range(ny // 2):
        one = one_in[edge + pair]
        two = two_in[edge + pair]
        below = jnp.where(even, two, one)
        above = jnp.where(even, one, two)
        tiles.append(jnp.where(lower, below, pltpu.roll(above, 8, 1)))
        tiles.append(jnp.where(lower, pltpu.roll(below, LANES - 8, 1), above))
    halo = jnp.concatenate(tiles, axis=0)
    operand = jnp.concatenate(halves(halo if first else 2.0 * halo), axis=1)
    for x in range(8):
        product = jnp.dot(operand, w_ref[x], preferred_element_type=F32)
        third = product[:, :LANES] + product[:, LANES:]
        for y in range(ny):
            here = pl.ds((y * 8 + x) * SUBS, SUBS)
            total = part_ref[here] + atoms_ref[here] + third[y * SUBS : (y + 1) * SUBS]
            if first:
                total = total + diag_ref[here] * z_ref[here]
            acc[here] = total
    if not last:

        def edges(pair, carry):
            rows = acc[pl.ds(pl.multiple_of(pair * LANES, LANES), LANES)]
            low, high = pack_edges([rows[SUBS * m : SUBS * (m + 1)] for m in range(16)], lane)
            one_ref[pair], two_ref[pair] = send_edges(even, low, high)
            return carry

        lax.fori_loop(0, ny // 2, edges, 0, unroll=4)
    if last:
        size = nb * 64
        for n in range(group // 2):
            for core in range(2):
                slot = (me_ref[0] // 2 ^ n) * 2 + core
                i, j = slot // gy, slot % gy
                for x in range(8):
                    rows = [
                        acc[pl.ds(((j * 8 + y) * 8 + x) * SUBS + i * nb, nb)] for y in range(8)
                    ]
                    if nb == 1:
                        turned = [jnp.concatenate(rows, axis=0)]
                    else:
                        turned = jnp.swapaxes(jnp.stack(rows, axis=0), 0, 1)
                    for b in range(nb):
                        at = core * size + b * 64 + x * 8
                        blocks[n][at : at + 8] = turned[b]


def turn(ref, first):
    return swapped(
        [ref[pl.ds(pl.multiple_of(first + 64 * s, SUBS), SUBS)] for s in range(SUBS)]
    )


def gather_kernel(group, nb, per_chunk, chunk, scale, me_ref, *refs):
    half = group // 2
    blocks, refs = refs[: half + 1], refs[half + 1 :]
    if chunk:
        earlier, refs = refs[:chunk], refs[chunk + 1 :]
    out_ref, gram_ref, field, sem = refs[0], refs[1], refs[-2], refs[-1]
    size = nb * 64
    rows = per_chunk * 64
    for slot, source in column_sources(
        me_ref[0], blocks[:half], blocks[half], size, me_ref[0] % 2
    ):
        field[pl.ds(pl.multiple_of(slot * size, 64), size)] = source[...]
    store = pltpu.make_async_copy(field, out_ref.at[pl.ds(chunk * rows, rows)], sem.at[0])
    store.start()
    gram_ref[...] = jnp.zeros_like(gram_ref)

    def cells(n, carry):
        total = None
        turned = [turn(field, g * SUBS * 64 + n * 8) for g in range(per_chunk // SUBS)]
        for m in range(4):
            pieces = []
            for c in range(2):
                cell = m * 2 + c
                pieces.append(jnp.concatenate([group_[cell] for group_ in turned], axis=0))
            both = jnp.concatenate(halves(jnp.concatenate(pieces, axis=1)), axis=0)
            if chunk < CHUNKS - 1:
                refs[2][n * 4 + m] = both
            against = [earlier[c][n * 4 + m] for c in range(chunk)] if chunk else []
            product = lax.dot_general(
                jnp.concatenate([*against, both], axis=0),
                both,
                (((1,), (1,)), ((), ())),
                preferred_element_type=F32,
            )
            total = product if total is None else total + product
        total = total[:, :per_chunk] + total[:, per_chunk:]
        for c in range(chunk + 1):
            first = 2 * c * per_chunk
            gram_ref[c] += (
                total[first : first + per_chunk]
                + total[first + per_chunk : first + 2 * per_chunk]
            )
        return carry

    lax.fori_loop(0, 8, cells, 0, unroll=2)
    gram_ref[...] *= scale
    store.wait()


def shape(*dims, dtype=F32):
    return jax.ShapeDtypeStruct(dims, dtype)


def cost(microseconds):
    return pl.CostEstimate(
        flops=int(microseconds * 1e9), bytes_accessed=int(microseconds * 3e6), transcendentals=0
    )


def shards(panel, potential, atom_corner, proj_index, projectors, couplings):
    bands, size_x, size_y, size_z = panel.shape
    count, nproj = couplings.shape
    gx, gy, gz = lax.axis_size("gx"), lax.axis_size("gy"), lax.axis_size("gz")
    group = gx * gy
    nb = bands // (CHUNKS * group)
    fold = 2 if gx == 2 else 1
    column = ("gx", "gy")
    me = lax.axis_index("gx") * gy + lax.axis_index("gy")
    me_z = lax.axis_index("gz")
    me_arr = jnp.stack([me, me_z % 2])
    rows = gy * 64
    pairs = gy * 4

    def swap(block, d):
        return lax.ppermute(block, column, [(s, s ^ d) for s in range(group)])

    def swap_z(block, d):
        return lax.ppermute(block, "gz", [(s, s ^ d) for s in range(gz)])

    anchor = jnp.stack(
        [
            lax.axis_index("gx") * size_x,
            lax.axis_index("gy") * size_y,
            me_z * size_z,
        ]
    )
    local = atom_corner - anchor[None, :]
    meta = jnp.concatenate([local[:, 1] * 8 + local[:, 0], local[:, 2]]).astype(F32)
    meta = jnp.broadcast_to(jnp.pad(meta, (0, LANES - 2 * count))[None], (8, LANES))
    part_rows = 64 + 4 * count + 8
    size = nb * 64
    tables = part_rows - 64
    core = me % 2

    def cross(blocks):
        return [blocks[0]] + [swap(blocks[n], 2 * n) for n in range(1, group // 2)]

    def beside(crossed):
        halves_of = [lax.dynamic_slice_in_dim(b, (1 - core) * size, size, 0) for b in crossed]
        return swap(jnp.concatenate(halves_of, axis=0), 1)

    field = panel.reshape(bands * 64, LANES)
    parts = pl.pallas_call(
        functools.partial(parts_kernel, count, fold),
        out_shape=shape(part_rows, LANES),
        in_specs=[VMEM] * 5,
        out_specs=VMEM,
        compiler_params=PARAMS,
        cost_estimate=cost(1),
        name="parts",
    )(
        proj_index,
        projectors,
        jnp.sqrt(couplings * (1.0 / HALF)).T,
        potential.reshape(64, LANES),
        meta,
    )
    rest = field.reshape(CHUNKS, group // 2, 2, size, LANES)
    passed = lax.dynamic_slice_in_dim(rest, 1 - core, 1, 2).reshape(-1, LANES)
    passed = swap(passed, 1)
    other_parts = swap(parts, 1)
    forward = []
    joined = []
    for chunk in range(CHUNKS):
        extra = (64, tables) if chunk == 0 else (0, 64 if chunk == CHUNKS - 1 else 0)
        joined = pl.pallas_call(
            functools.partial(join_kernel, group, size, chunk, extra),
            out_shape=[shape(2 * size + 2 * extra[1], LANES)] * (group // 2),
            in_specs=[SMEM, HBM, ANY] + [VMEM] * 3,
            out_specs=[VMEM] * (group // 2),
            scratch_shapes=[pltpu.SemaphoreType.DMA((1,))],
            compiler_params=PARAMS,
            cost_estimate=cost(1),
            name="join",
        )(me_arr, field, forward[0][1] if chunk else parts, passed, parts, other_parts)
        forward.append(cross(joined))

    tile_shape = shape(rows * SUBS, LANES)
    edge_shape = shape(pairs, SUBS, LANES)
    def unpack(chunk, after):
        tiles, one, two = pl.pallas_call(
            functools.partial(unpack_kernel, gx, gy, nb),
            out_shape=[tile_shape, edge_shape, edge_shape],
            in_specs=[SMEM, ANY] + [VMEM] * len(forward[chunk]),
            out_specs=[VMEM] * 3,
            compiler_params=PARAMS,
            cost_estimate=cost(2),
            name="unpack",
        )(me_arr, after, *forward[chunk])
        return None, tiles, one, two

    states = [unpack(0, joined[0])]
    root_tiles = group * count * 8 // (2 * fold)
    roots, places = pl.pallas_call(
        functools.partial(atoms_kernel, gx, gy, nb, count, fold),
        out_shape=[
            shape(root_tiles, SUBS, LANES),
            shape(2 * group * count, dtype=jnp.int32),
        ],
        in_specs=[SMEM, ANY] + [VMEM] * (group // 2),
        out_specs=[VMEM, SMEM],
        scratch_shapes=[
            pltpu.SMEM((group * 8, LANES), F32),
            pltpu.SemaphoreType.DMA((1,)),
        ],
        compiler_params=PARAMS,
        cost_estimate=cost(1),
        name="atoms",
    )(me_arr, states[0][2], *forward[0])
    for chunk in range(1, CHUNKS):
        states.append(unpack(chunk, roots))
    diag = pl.pallas_call(
        functools.partial(diagonal_kernel, gx, gy, nb),
        out_shape=tile_shape,
        in_specs=[SMEM, ANY] + [VMEM] * (group // 2),
        out_specs=VMEM,
        compiler_params=PARAMS,
        cost_estimate=cost(1),
        name="diagonal",
    )(me_arr, states[-1][2], *forward[-1])

    own_weights, halo_weights = (jnp.asarray(w) for w in line_weights())
    summing = np.kron(np.eye(2 * fold), np.ones((TILE // fold, TILE // fold)))
    summing = jnp.asarray(np.concatenate([summing, summing], axis=0).astype(ml_dtypes.bfloat16))
    pair_one = [(s, s ^ 1) for s in range(gz)]
    pair_two = [(s, (s + (1 if s % 2 else -1)) % gz) for s in range(gz)]

    results = [None] * CHUNKS
    for degree_step in range(DEGREE):
        first, last = degree_step == 0, degree_step == DEGREE - 1
        if first:
            halos = [
                (lax.ppermute(state[2], "gz", pair_one), lax.ppermute(state[3], "gz", pair_two))
                for state in states
            ]
        else:
            one = jnp.concatenate([state[2] for state in states], axis=0)
            two = jnp.concatenate([state[3] for state in states], axis=0)
            halos = [(lax.ppermute(one, "gz", pair_one), lax.ppermute(two, "gz", pair_two))] * CHUNKS
        inner = []
        for prev, tiles, _, _ in states:
            operands = [roots, places, tiles]
            if not first:
                operands += [prev, diag]
            operands += [roots, own_weights, summing]
            inner.append(
                pl.pallas_call(
                    functools.partial(inner_kernel, gx, gy, nb, count, fold, first),
                    out_shape=[tile_shape, tile_shape],
                    in_specs=[ANY, SMEM] + [VMEM] * (len(operands) - 2),
                    out_specs=[VMEM] * 2,
                    scratch_shapes=[pltpu.VMEM((rows * SUBS, LANES), F32)]
                    + [pltpu.VMEM((root_tiles // 8, SUBS, LANES), F32)] * 2,
                    compiler_params=PARAMS,
                    cost_estimate=cost(4),
                    name="inner",
                )(*operands)
            )
        for chunk, (_, tiles, _, _) in enumerate(states):
            edge = 0 if first else chunk * pairs
            after = roots if first else inner[chunk - 1][0]
            operands = [me_arr, after, *inner[chunk], *halos[chunk]]
            operands.append(halo_weights)
            if first:
                operands += [tiles, diag]
            outs = pl.pallas_call(
                functools.partial(outer_kernel, gx, gy, nb, first, last, edge),
                out_shape=[shape(2 * size, LANES)] * (group // 2)
                if last
                else [tile_shape, edge_shape, edge_shape],
                in_specs=[SMEM, ANY] + [VMEM] * (len(operands) - 2),
                out_specs=[VMEM] * (group // 2 if last else 3),
                scratch_shapes=[pltpu.VMEM((rows * SUBS, LANES), F32)] * last,
                compiler_params=PARAMS,
                cost_estimate=cost(1),
                name="outer",
            )(*operands)
            if last:
                crossed = cross(outs)
                results[chunk] = crossed + [beside(crossed)]
            else:
                states[chunk] = (tiles, *outs)

    total_cells = size_x * size_y * size_z * group * gz
    per_chunk = bands // CHUNKS
    filtered, kept, gram_columns = None, [], []
    for chunk, blocks in enumerate(results):
        operands = [me_arr, *blocks, *kept] + ([filtered] if chunk else [])
        filtered, columns, *own = pl.pallas_call(
            functools.partial(gather_kernel, group, nb, per_chunk, chunk, 1.0 / total_cells),
            out_shape=[
                shape(bands * 64, LANES),
                shape(chunk + 1, per_chunk, per_chunk),
            ]
            + [shape(32, 2 * per_chunk, 2 * LANES, dtype=BF16)] * (chunk < CHUNKS - 1),
            in_specs=[SMEM] + [VMEM] * (len(operands) - 1 - (chunk > 0)) + [ANY] * (chunk > 0),
            out_specs=[ANY, VMEM] + [VMEM] * (chunk < CHUNKS - 1),
            scratch_shapes=[
                pltpu.VMEM((per_chunk * 64, LANES), F32),
                pltpu.SemaphoreType.DMA((1,)),
            ],
            input_output_aliases={len(operands) - 1: 0} if chunk else {},
            compiler_params=PARAMS,
            cost_estimate=cost(2),
            name="gather",
        )(*operands)
        kept += own
        gram_columns.append(columns)
    gram = jnp.concatenate(
        [
            jnp.concatenate(
                [gram_columns[d][c] if c <= d else gram_columns[c][d].T for d in range(CHUNKS)],
                axis=1,
            )
            for c in range(CHUNKS)
        ],
        axis=0,
    )

    gram = gram + swap(gram, 1)
    d = 2
    while d < group:
        if 2 * d < group:
            gram = gram + (swap(gram, d) + swap(gram, 2 * d) + swap(gram, 3 * d))
        else:
            gram = gram + swap(gram, d)
        d *= 4
    share = bands // gz
    terms = []
    for d in range(gz):
        term = lax.dynamic_slice_in_dim(gram, (me_z ^ d) * share, share, 0)
        terms.append(swap_z(term, d) if d else term)
    return filtered.reshape(panel.shape), sum(terms[1:], terms[0])


def solution(mesh):
    placed = (
        P(None, "gx", "gy", "gz"),
        P("gx", "gy", "gz"),
        P(("gx", "gy", "gz"), None),
        P(("gx", "gy", "gz"), None),
        P(("gx", "gy", "gz"), None, None),
        P(("gx", "gy", "gz"), None),
    )
    return jax.shard_map(
        shards,
        mesh=mesh,
        in_specs=placed,
        out_specs=(P(None, "gx", "gy", "gz"), P("gz", None)),
        check_vma=False,
    )
```

```python
import functools
import math

import jax
import jax.numpy as jnp
import ml_dtypes
import numpy as np
from jax import lax
from jax.experimental import pallas as pl
from jax.experimental.pallas import tpu as pltpu
from jax.sharding import PartitionSpec as P

DEGREE = 4
CHUNKS = 2

STENCIL = (
    -5369.0 / 1800.0,
    12.0 / 7.0,
    -15.0 / 56.0,
    10.0 / 189.0,
    -1.0 / 112.0,
    2.0 / 1925.0,
    -1.0 / 16632.0,
)
SPACING = 0.224
CENTER = 210.5
HALF = 209.5
REACH = 6
TILE = 64
LANES = 128
SUBS = 8
KINETIC = -0.5 / (SPACING * SPACING) / HALF
TAPS = tuple(KINETIC * c for c in STENCIL)
DIAGONAL = 3.0 * TAPS[0] - CENTER / HALF

F32 = jnp.float32
BF16 = jnp.bfloat16
VMEM = pl.BlockSpec(memory_space=pltpu.VMEM)
SMEM = pl.BlockSpec(memory_space=pltpu.SMEM)
ANY = pl.BlockSpec(memory_space=pl.ANY)
HBM = pl.BlockSpec(memory_space=pltpu.HBM)


PARAMS = pltpu.CompilerParams(vmem_limit_bytes=24 << 20)


def split_halves(matrix):
    high = matrix.astype(ml_dtypes.bfloat16)
    low = (matrix - high.astype(np.float64)).astype(ml_dtypes.bfloat16)
    wide = np.concatenate([high, low], axis=1)
    return np.concatenate([wide, wide], axis=0)


def line_weights():
    own = np.zeros((LANES, LANES))
    halo = np.zeros((8, LANES, LANES))
    for k in range(1, REACH + 1):
        for z in range(LANES):
            for cell in (z + k, z - k):
                if 0 <= cell < LANES:
                    own[cell, z] = TAPS[k]
                else:
                    lane = 8 + cell - LANES if cell >= LANES else 8 + cell
                    for slot in range(8):
                        halo[slot, 16 * slot + lane, z] = TAPS[k]
    return split_halves(own), np.stack([split_halves(slot) for slot in halo])


def halves(value):
    high = value.astype(BF16)
    low = (value - high.astype(F32)).astype(BF16)
    return high, low


def parts_kernel(count, fold, index_ref, proj_ref, root_ref, pot_ref, meta_ref, out_ref):
    out_ref[0:64, :] = pot_ref[...]
    point = lax.broadcasted_iota(jnp.int32, (TILE, TILE), 0)
    width = TILE // fold
    sorted_rows = []
    for atom in range(count):
        order = index_ref[atom : atom + 1, :]
        if fold == 2:
            order = ((order >> 4) & 1) * width + (order >> 5) * 16 + (order & 15)
        hot = (point == order).astype(F32)
        sorted_rows.append(
            lax.dot_general(
                proj_ref[atom],
                hot,
                (((1,), (1,)), ((), ())),
                precision=lax.Precision.HIGHEST,
                preferred_element_type=F32,
            )
            * root_ref[:, atom : atom + 1]
        )
    row = 64
    for first in range(0, count, 2 * fold):
        for f in range(fold):
            out_ref[row : row + 8, :] = jnp.concatenate(
                [sorted_rows[first + q][:, f * width : (f + 1) * width] for q in range(2 * fold)],
                axis=1,
            )
            row += 8
    out_ref[row : row + 8, :] = meta_ref[...]


def swapped(rows):
    if len(rows) == 1:
        return [rows[0][y : y + 1] for y in range(8)]
    return jnp.swapaxes(jnp.stack(rows, axis=0), 0, 1)


def column_sources(me, crossed, beside, size, core):
    pairs = []
    for n, block in enumerate(crossed):
        pairs.append((me ^ (2 * n), block.at[pl.ds(pl.multiple_of(core * size, 8), size)]))
        pairs.append((me ^ (2 * n) ^ 1, beside.at[pl.ds(n * size, size)]))
    return pairs


def atoms_kernel(gx, gy, nb, count, fold, me_ref, after_ref, *refs):
    half = gx * gy // 2
    roots_ref, meta_ref, whole, raw, sem = refs[half:]
    rows = 4 * count + 8
    sources = []
    for n in range(half):
        for other in range(2):
            at = 2 * nb * 64 + other * rows
            sources.append((me_ref[0] ^ (2 * n + other), refs[n].at[pl.ds(at, rows)]))
    for slot, source in sources:
        whole[pl.ds(slot, 1)] = source[rows - 8 : rows - 7].astype(jnp.int32)
    copy = pltpu.make_async_copy(whole, raw, sem.at[0])
    copy.start()
    sub = lax.broadcasted_iota(jnp.int32, (SUBS, LANES), 0)
    per_slot = count // (2 * fold)
    for slot, source in sources:
        for m in range(per_slot):
            for k in range(8):
                parts = []
                for f in range(fold):
                    at = (m * fold + f) * 8 + k
                    parts.append(jnp.broadcast_to(source[at : at + 1, :], (SUBS, LANES)))
                value = parts[0] if fold == 1 else jnp.where(sub < SUBS // 2, parts[0], parts[1])
                roots_ref[(slot * per_slot + m) * 8 + k] = value
    copy.wait()

    def corners(slot, carry):
        for atom in range(count):
            meta_ref[2 * (slot * count + atom)] = raw[slot, atom]
            meta_ref[2 * (slot * count + atom) + 1] = raw[slot, count + atom]
        return carry

    lax.fori_loop(0, gx * gy, corners, 0)


def diagonal_kernel(gx, gy, nb, me_ref, after_ref, *refs):
    half = gx * gy // 2
    diag_ref = refs[half]
    for n in range(half):
        for other in range(2):
            slot = me_ref[0] ^ (2 * n + other)
            i, j = slot // gy, slot % gy
            for x in range(8):
                first = 2 * nb * 64 + other * 64 + x * 8
                value = refs[n][first : first + 8, :] * (1.0 / HALF) + DIAGONAL
                for y in range(8):
                    at = ((j * 8 + y) * 8 + x) * SUBS + i * nb
                    diag_ref[pl.ds(at, nb)] = jnp.broadcast_to(value[y : y + 1], (nb, LANES))


def pack_edges(values, lane):
    wide = []
    for first in (0, 8):
        tile = None
        for slot in range(8):
            moved = pltpu.roll(values[first + slot], (16 * slot + 2 + REACH) % LANES, 1)
            tile = moved if tile is None else jnp.where((lane >> 4) == slot, moved, tile)
        wide.append(tile)
    lower = (lane & 15) < 8
    low = jnp.where(lower, pltpu.roll(wide[0], LANES - 8, 1), wide[1])
    high = jnp.where(lower, wide[0], pltpu.roll(wide[1], 8, 1))
    return low, high


def send_edges(even, low, high):
    return jnp.where(even, high, low), jnp.where(even, low, high)


def join_kernel(
    group, size, chunk, extra, chips, me_ref, field, after_ref, passed, own_ref, other_ref, *refs
):
    blocks, sem = refs[:-1], refs[-1]
    copies = []
    for n, block in zip(chips, blocks):
        chip = me_ref[0] // 2 ^ n
        row = (chunk * group + chip * 2 + me_ref[0] % 2) * size
        copies.append(
            pltpu.make_async_copy(
                field.at[pl.ds(pl.multiple_of(row, 64), size)],
                block.at[pl.ds(0, size)],
                sem.at[0],
            )
        )
    for copy in copies:
        copy.start()
    first, rows = extra
    for n, block in zip(chips, blocks):
        chip = me_ref[0] // 2 ^ n
        row = (chunk * group // 2 + chip) * size
        block[pl.ds(size, size)] = passed[pl.ds(pl.multiple_of(row, 64), size)]
        if rows:
            block[pl.ds(2 * size, rows)] = own_ref[pl.ds(first, rows)]
            block[pl.ds(2 * size + rows, rows)] = other_ref[pl.ds(first, rows)]
    for copy in copies:
        copy.wait()


def unpack_kernel(gx, gy, nb, me_ref, after_ref, *refs):
    half = gx * gy // 2
    size = nb * 64
    z_ref, one_ref, two_ref = refs[-3:]
    for n in range(half):
        for other in range(2):
            slot = me_ref[0] ^ (2 * n + other)
            i, j = slot // gy, slot % gy
            for x in range(8):
                first = x * 8 + other * size
                turned = swapped([refs[n][first + b * 64 : first + b * 64 + 8] for b in range(nb)])
                for y in range(8):
                    z_ref[pl.ds(((j * 8 + y) * 8 + x) * SUBS + i * nb, nb)] = turned[y]
    lane = lax.broadcasted_iota(jnp.int32, (SUBS, LANES), 1)
    even = me_ref[1] == 0

    def lines(pair, carry):
        tiles = z_ref[pl.ds(pl.multiple_of(pair * LANES, LANES), LANES)]
        values = [tiles[SUBS * q : SUBS * (q + 1)] for q in range(16)]
        low, high = pack_edges(values, lane)
        one_ref[pair], two_ref[pair] = send_edges(even, low, high)
        return carry

    lax.fori_loop(0, gy * 4, lines, 0, unroll=4)


def tile_rows(row):
    return pl.ds(pl.multiple_of(row * SUBS, SUBS), SUBS)


def inner_kernel(gx, gy, nb, count, fold, first, after_ref, meta_ref, *refs):
    if first:
        z_ref, roots_ref, w_ref, sum_ref = refs[:4]
    else:
        z_ref, prev_ref, diag_ref, roots_ref, w_ref, sum_ref = refs[:6]
    out_ref, atoms_ref, tile_ref, spread_ref = refs[-4:]
    group = gx * gy
    ny = gy * 8
    width = TILE // fold
    per_tile = 2 * fold
    per_slot = count // per_tile
    lane = lax.broadcasted_iota(jnp.int32, (SUBS, LANES), 1)
    sub = lax.broadcasted_iota(jnp.int32, (SUBS, LANES), 0)

    def tile_row(t):
        return ((t % 4) * 8 + (t // 4) * fold) * SUBS

    def gather(slot):
        for m in range(per_slot):
            tile = jnp.zeros((SUBS, LANES), F32)
            for q in range(per_tile):
                n = slot * count + per_tile * m + q
                start = meta_ref[2 * n]
                back = LANES - meta_ref[2 * n + 1]
                for t in range(16 // fold):
                    value = z_ref[pl.ds(start + tile_row(t), SUBS)]
                    if fold == 2:
                        beyond = z_ref[pl.ds(start + (tile_row(t) + nb), SUBS)]
                        value = jnp.where(sub < nb, value, beyond)
                    value = pltpu.roll(value, back + (4 * t + width * q), 1)
                    tile = jnp.where((lane >> 2) == t + q * (width // 4), value, tile)
            tile_ref[slot * per_slot + m] = tile

    def scatter(slot, i):
        for m in range(per_slot):
            spread = spread_ref[slot * per_slot + m]
            for q in range(per_tile):
                n = slot * count + per_tile * m + q
                start = meta_ref[2 * n]
                z0 = meta_ref[2 * n + 1]
                inside = (lane >= z0) & (lane < z0 + 4)
                if fold == 1:
                    masks = [inside & (sub // nb == i)]
                else:
                    masks = [inside & (sub < nb), inside & (sub >= nb)]
                sums = []
                for t in range(16 // fold):
                    value = pltpu.roll(spread, z0 + (LANES - 4 * t - width * q), 1)
                    for f, mask in enumerate(masks):
                        here = pl.ds(start + (tile_row(t) + f * nb), SUBS)
                        sums.append((here, atoms_ref[here] + jnp.where(mask, value, 0.0)))
                for here, value in sums:
                    atoms_ref[here] = value

    def third_dim(n, carry):
        for c in range(group // 8):
            gather(n * (group // 8) + c)
        block = pl.ds(pl.multiple_of(n * 32 * SUBS, 32 * SUBS), 32 * SUBS)
        operand = jnp.concatenate(halves(z_ref[block]), axis=1)
        product = jnp.dot(operand, w_ref[...], preferred_element_type=F32)
        out_ref[block] = product[:, :LANES] + product[:, LANES:]
        atoms_ref[block] = jnp.zeros((32 * SUBS, LANES), F32)
        return carry

    lax.fori_loop(0, 8, third_dim, 0, unroll=8 if group <= 8 else 1)

    def contract(eight, carry):
        products = []
        for m in range(8):
            tile = tile_ref[eight * 8 + m]
            for k in range(8):
                products.append(tile * roots_ref[(eight * 8 + m) * 8 + k])
        sums = jnp.dot(
            jnp.concatenate(halves(jnp.concatenate(products, axis=0)), axis=1),
            sum_ref[...],
            preferred_element_type=F32,
        )
        for m in range(8):
            spread = None
            for k in range(8):
                at = (m * 8 + k) * SUBS
                coeff = sums[at : at + SUBS]
                if fold == 2:
                    coeff = coeff + pltpu.roll(coeff, nb, 0)
                term = coeff * roots_ref[(eight * 8 + m) * 8 + k]
                spread = term if spread is None else spread + term
            spread_ref[eight * 8 + m] = spread if first else 2.0 * spread
        return carry

    lax.fori_loop(0, group * per_slot // 8, contract, 0, unroll=2)

    def rest(four):
        for q in range(4):
            y = four * 4 + q
            values = [z_ref[tile_rows(y * 8 + x)] for x in range(8)]
            after = [pltpu.roll(value, SUBS - nb, 0) for value in values]
            before = after if gx == 2 else [pltpu.roll(value, nb, 0) for value in values]
            wide = before + values + after
            up = [(y + k) % ny * 8 for k in range(REACH + 1)]
            down = [(y + ny - k) % ny * 8 for k in range(REACH + 1)]
            for x in range(8):
                here = tile_rows(y * 8 + x)
                total = out_ref[here]
                if not first:
                    total = total + diag_ref[here] * values[x]
                for k in range(1, REACH + 1):
                    beside = z_ref[tile_rows(up[k] + x)] + z_ref[tile_rows(down[k] + x)]
                    total = total + TAPS[k] * (wide[8 + x + k] + wide[8 + x - k] + beside)
                if not first:
                    total = 2.0 * total - prev_ref[here]
                out_ref[here] = total

    def block(j, carry):
        for half in range(2):
            for i in range(half * gx // 2, (half + 1) * gx // 2):
                scatter(i * gy + j, i)
            rest(2 * j + half)
        return carry

    lax.fori_loop(0, gy, block, 0, unroll=gy if group <= 8 else 1)


def outer_kernel(
    gx, gy, nb, first, last, edge, me_ref, after_ref, part_ref, atoms_ref, one_in, two_in, w_ref, *refs
):
    group = gx * gy
    if first:
        z_ref, diag_ref, refs = refs[0], refs[1], refs[2:]
    if last:
        blocks, acc = refs[: group // 2], refs[group // 2]
    else:
        acc, one_ref, two_ref = refs
    lane = lax.broadcasted_iota(jnp.int32, (SUBS, LANES), 1)
    even = me_ref[1] == 0
    lower = (lane & 15) < 8
    ny = gy * 8
    tiles = []
    for pair in range(ny // 2):
        one = one_in[edge + pair]
        two = two_in[edge + pair]
        below = jnp.where(even, two, one)
        above = jnp.where(even, one, two)
        tiles.append(jnp.where(lower, below, pltpu.roll(above, 8, 1)))
        tiles.append(jnp.where(lower, pltpu.roll(below, LANES - 8, 1), above))
    halo = jnp.concatenate(tiles, axis=0)
    operand = jnp.concatenate(halves(halo if first else 2.0 * halo), axis=1)
    for x in range(8):
        product = jnp.dot(operand, w_ref[x], preferred_element_type=F32)
        third = product[:, :LANES] + product[:, LANES:]
        for y in range(ny):
            here = pl.ds((y * 8 + x) * SUBS, SUBS)
            total = part_ref[here] + atoms_ref[here] + third[y * SUBS : (y + 1) * SUBS]
            if first:
                total = total + diag_ref[here] * z_ref[here]
            acc[here] = total
    if not last:

        def edges(pair, carry):
            rows = acc[pl.ds(pl.multiple_of(pair * LANES, LANES), LANES)]
            low, high = pack_edges([rows[SUBS * m : SUBS * (m + 1)] for m in range(16)], lane)
            one_ref[pair], two_ref[pair] = send_edges(even, low, high)
            return carry

        lax.fori_loop(0, ny // 2, edges, 0, unroll=4)
    if last:
        size = nb * 64
        for n in range(group // 2):
            for core in range(2):
                slot = (me_ref[0] // 2 ^ n) * 2 + core
                i, j = slot // gy, slot % gy
                for x in range(8):
                    rows = [
                        acc[pl.ds(((j * 8 + y) * 8 + x) * SUBS + i * nb, nb)] for y in range(8)
                    ]
                    if nb == 1:
                        turned = [jnp.concatenate(rows, axis=0)]
                    else:
                        turned = jnp.swapaxes(jnp.stack(rows, axis=0), 0, 1)
                    for b in range(nb):
                        at = core * size + b * 64 + x * 8
                        blocks[n][at : at + 8] = turned[b]


def turn(ref, first):
    return swapped(
        [ref[pl.ds(pl.multiple_of(first + 64 * s, SUBS), SUBS)] for s in range(SUBS)]
    )


def gather_kernel(group, nb, per_chunk, chunk, scale, me_ref, *refs):
    half = group // 2
    blocks, refs = refs[: half + 1], refs[half + 1 :]
    if chunk:
        earlier, refs = refs[:chunk], refs[chunk + 1 :]
    out_ref, gram_ref, field, sem = refs[0], refs[1], refs[-2], refs[-1]
    size = nb * 64
    rows = per_chunk * 64
    for slot, source in column_sources(
        me_ref[0], blocks[:half], blocks[half], size, me_ref[0] % 2
    ):
        field[pl.ds(pl.multiple_of(slot * size, 64), size)] = source[...]
    store = pltpu.make_async_copy(field, out_ref.at[pl.ds(chunk * rows, rows)], sem.at[0])
    store.start()
    gram_ref[...] = jnp.zeros_like(gram_ref)

    def cells(n, carry):
        total = None
        turned = [turn(field, g * SUBS * 64 + n * 8) for g in range(per_chunk // SUBS)]
        for m in range(4):
            pieces = []
            for c in range(2):
                cell = m * 2 + c
                pieces.append(jnp.concatenate([group_[cell] for group_ in turned], axis=0))
            both = jnp.concatenate(halves(jnp.concatenate(pieces, axis=1)), axis=0)
            if chunk < CHUNKS - 1:
                refs[2][n * 4 + m] = both
            against = [earlier[c][n * 4 + m] for c in range(chunk)] if chunk else []
            product = lax.dot_general(
                jnp.concatenate([*against, both], axis=0),
                both,
                (((1,), (1,)), ((), ())),
                preferred_element_type=F32,
            )
            total = product if total is None else total + product
        total = total[:, :per_chunk] + total[:, per_chunk:]
        for c in range(chunk + 1):
            first = 2 * c * per_chunk
            gram_ref[c] += (
                total[first : first + per_chunk]
                + total[first + per_chunk : first + 2 * per_chunk]
            )
        return carry

    lax.fori_loop(0, 8, cells, 0, unroll=2)
    gram_ref[...] *= scale
    store.wait()


def shape(*dims, dtype=F32):
    return jax.ShapeDtypeStruct(dims, dtype)


def cost(microseconds):
    return pl.CostEstimate(
        flops=int(microseconds * 1e9), bytes_accessed=int(microseconds * 3e6), transcendentals=0
    )


def shards(panel, potential, atom_corner, proj_index, projectors, couplings):
    bands, size_x, size_y, size_z = panel.shape
    count, nproj = couplings.shape
    gx, gy, gz = lax.axis_size("gx"), lax.axis_size("gy"), lax.axis_size("gz")
    group = gx * gy
    nb = bands // (CHUNKS * group)
    fold = 2 if gx == 2 else 1
    column = ("gx", "gy")
    me = lax.axis_index("gx") * gy + lax.axis_index("gy")
    me_z = lax.axis_index("gz")
    me_arr = jnp.stack([me, me_z % 2])
    rows = gy * 64
    pairs = gy * 4

    def swap(block, d):
        return lax.ppermute(block, column, [(s, s ^ d) for s in range(group)])

    def swap_z(block, d):
        return lax.ppermute(block, "gz", [(s, s ^ d) for s in range(gz)])

    anchor = jnp.stack(
        [
            lax.axis_index("gx") * size_x,
            lax.axis_index("gy") * size_y,
            me_z * size_z,
        ]
    )
    local = atom_corner - anchor[None, :]
    start = (me % gy * 64 + local[:, 1] * 8 + local[:, 0]) * SUBS
    if fold == 2:
        start = start + me // gy * nb
    meta = jnp.concatenate([start, local[:, 2]]).astype(F32)
    meta = jnp.broadcast_to(jnp.pad(meta, (0, LANES - 2 * count))[None], (8, LANES))
    part_rows = 64 + 4 * count + 8
    size = nb * 64
    tables = part_rows - 64
    core = me % 2

    def cross(blocks):
        return [blocks[0]] + [swap(blocks[n], 2 * n) for n in range(1, group // 2)]

    def beside(crossed):
        halves_of = [lax.dynamic_slice_in_dim(b, (1 - core) * size, size, 0) for b in crossed]
        return swap(jnp.concatenate(halves_of, axis=0), 1)

    field = panel.reshape(bands * 64, LANES)
    parts = pl.pallas_call(
        functools.partial(parts_kernel, count, fold),
        out_shape=shape(part_rows, LANES),
        in_specs=[VMEM] * 5,
        out_specs=VMEM,
        compiler_params=PARAMS,
        cost_estimate=cost(1),
        name="parts",
    )(
        proj_index,
        projectors,
        jnp.sqrt(couplings * (1.0 / HALF)).T,
        potential.reshape(64, LANES),
        meta,
    )
    rest = field.reshape(CHUNKS, group // 2, 2, size, LANES)
    passed = lax.dynamic_slice_in_dim(rest, 1 - core, 1, 2).reshape(-1, LANES)
    passed = swap(passed, 1)
    other_parts = swap(parts, 1)
    forward = []
    for chunk in range(CHUNKS):
        extra = (64, tables) if chunk == 0 else (0, 64 if chunk == CHUNKS - 1 else 0)

        def join(chips, after):
            return pl.pallas_call(
                functools.partial(join_kernel, group, size, chunk, extra, chips),
                out_shape=[shape(2 * size + 2 * extra[1], LANES)] * len(chips),
                in_specs=[SMEM, HBM, ANY] + [VMEM] * 3,
                out_specs=[VMEM] * len(chips),
                scratch_shapes=[pltpu.SemaphoreType.DMA((1,))],
                compiler_params=PARAMS,
                cost_estimate=cost(1),
                name="join",
            )(me_arr, field, after, passed, parts, other_parts)

        sent = join(range(1, group // 2), forward[0][1] if chunk else parts)
        came = [swap(block, 2 * n) for n, block in enumerate(sent, 1)]
        forward.append([*join(range(1), came[0]), *came])

    tile_shape = shape(rows * SUBS, LANES)
    edge_shape = shape(pairs, SUBS, LANES)
    def unpack(chunk, after):
        tiles, one, two = pl.pallas_call(
            functools.partial(unpack_kernel, gx, gy, nb),
            out_shape=[tile_shape, edge_shape, edge_shape],
            in_specs=[SMEM, ANY] + [VMEM] * len(forward[chunk]),
            out_specs=[VMEM] * 3,
            compiler_params=PARAMS,
            cost_estimate=cost(2),
            name="unpack",
        )(me_arr, after, *forward[chunk])
        return None, tiles, one, two

    states = [unpack(0, sent[0])]
    root_tiles = group * count * 8 // (2 * fold)
    roots, places = pl.pallas_call(
        functools.partial(atoms_kernel, gx, gy, nb, count, fold),
        out_shape=[
            shape(root_tiles, SUBS, LANES),
            shape(2 * group * count, dtype=jnp.int32),
        ],
        in_specs=[SMEM, ANY] + [VMEM] * (group // 2),
        out_specs=[VMEM, SMEM],
        scratch_shapes=[
            pltpu.VMEM((group, LANES), jnp.int32),
            pltpu.SMEM((group, LANES), jnp.int32),
            pltpu.SemaphoreType.DMA((1,)),
        ],
        compiler_params=PARAMS,
        cost_estimate=cost(1),
        name="atoms",
    )(me_arr, states[0][2], *forward[0])
    for chunk in range(1, CHUNKS):
        states.append(unpack(chunk, roots))
    diag = pl.pallas_call(
        functools.partial(diagonal_kernel, gx, gy, nb),
        out_shape=tile_shape,
        in_specs=[SMEM, ANY] + [VMEM] * (group // 2),
        out_specs=VMEM,
        compiler_params=PARAMS,
        cost_estimate=cost(1),
        name="diagonal",
    )(me_arr, states[-1][2], *forward[-1])

    own_weights, halo_weights = (jnp.asarray(w) for w in line_weights())
    summing = np.kron(np.eye(2 * fold), np.ones((TILE // fold, TILE // fold)))
    summing = jnp.asarray(np.concatenate([summing, summing], axis=0).astype(ml_dtypes.bfloat16))
    pair_one = [(s, s ^ 1) for s in range(gz)]
    pair_two = [(s, (s + (1 if s % 2 else -1)) % gz) for s in range(gz)]

    results = [None] * CHUNKS
    for degree_step in range(DEGREE):
        first, last = degree_step == 0, degree_step == DEGREE - 1
        if first:
            halos = [
                (lax.ppermute(state[2], "gz", pair_one), lax.ppermute(state[3], "gz", pair_two))
                for state in states
            ]
        else:
            one = jnp.concatenate([state[2] for state in states], axis=0)
            two = jnp.concatenate([state[3] for state in states], axis=0)
            halos = [(lax.ppermute(one, "gz", pair_one), lax.ppermute(two, "gz", pair_two))] * CHUNKS
        inner = []
        for prev, tiles, _, _ in states:
            operands = [roots, places, tiles]
            if not first:
                operands += [prev, diag]
            operands += [roots, own_weights, summing]
            inner.append(
                pl.pallas_call(
                    functools.partial(inner_kernel, gx, gy, nb, count, fold, first),
                    out_shape=[tile_shape, tile_shape],
                    in_specs=[ANY, SMEM] + [VMEM] * (len(operands) - 2),
                    out_specs=[VMEM] * 2,
                    scratch_shapes=[pltpu.VMEM((root_tiles // 8, SUBS, LANES), F32)] * 2,
                    compiler_params=PARAMS,
                    cost_estimate=cost(4),
                    name="inner",
                )(*operands)
            )
        for chunk, (_, tiles, _, _) in enumerate(states):
            edge = 0 if first else chunk * pairs
            after = roots if first else inner[chunk - 1][0]
            operands = [me_arr, after, *inner[chunk], *halos[chunk]]
            operands.append(halo_weights)
            if first:
                operands += [tiles, diag]
            outs = pl.pallas_call(
                functools.partial(outer_kernel, gx, gy, nb, first, last, edge),
                out_shape=[shape(2 * size, LANES)] * (group // 2)
                if last
                else [tile_shape, edge_shape, edge_shape],
                in_specs=[SMEM, ANY] + [VMEM] * (len(operands) - 2),
                out_specs=[VMEM] * (group // 2 if last else 3),
                scratch_shapes=[pltpu.VMEM((rows * SUBS, LANES), F32)] * last,
                compiler_params=PARAMS,
                cost_estimate=cost(1),
                name="outer",
            )(*operands)
            if last:
                crossed = cross(outs)
                results[chunk] = crossed + [beside(crossed)]
            else:
                states[chunk] = (tiles, *outs)

    total_cells = size_x * size_y * size_z * group * gz
    per_chunk = bands // CHUNKS
    filtered, kept, gram_columns = None, [], []
    for chunk, blocks in enumerate(results):
        operands = [me_arr, *blocks, *kept] + ([filtered] if chunk else [])
        filtered, columns, *own = pl.pallas_call(
            functools.partial(gather_kernel, group, nb, per_chunk, chunk, 1.0 / total_cells),
            out_shape=[
                shape(bands * 64, LANES),
                shape(chunk + 1, per_chunk, per_chunk),
            ]
            + [shape(32, 2 * per_chunk, 2 * LANES, dtype=BF16)] * (chunk < CHUNKS - 1),
            in_specs=[SMEM] + [VMEM] * (len(operands) - 1 - (chunk > 0)) + [ANY] * (chunk > 0),
            out_specs=[ANY, VMEM] + [VMEM] * (chunk < CHUNKS - 1),
            scratch_shapes=[
                pltpu.VMEM((per_chunk * 64, LANES), F32),
                pltpu.SemaphoreType.DMA((1,)),
            ],
            input_output_aliases={len(operands) - 1: 0} if chunk else {},
            compiler_params=PARAMS,
            cost_estimate=cost(2),
            name="gather",
        )(*operands)
        kept += own
        gram_columns.append(columns)
    gram = jnp.concatenate(
        [
            jnp.concatenate(
                [gram_columns[d][c] if c <= d else gram_columns[c][d].T for d in range(CHUNKS)],
                axis=1,
            )
            for c in range(CHUNKS)
        ],
        axis=0,
    )

    gram = gram + swap(gram, 1)
    d = 2
    while d < group:
        if 2 * d < group:
            gram = gram + (swap(gram, d) + swap(gram, 2 * d) + swap(gram, 3 * d))
        else:
            gram = gram + swap(gram, d)
        d *= 4
    share = bands // gz
    terms = []
    for d in range(gz):
        term = lax.dynamic_slice_in_dim(gram, (me_z ^ d) * share, share, 0)
        terms.append(swap_z(term, d) if d else term)
    return filtered.reshape(panel.shape), sum(terms[1:], terms[0])


def solution(mesh):
    placed = (
        P(None, "gx", "gy", "gz"),
        P("gx", "gy", "gz"),
        P(("gx", "gy", "gz"), None),
        P(("gx", "gy", "gz"), None),
        P(("gx", "gy", "gz"), None, None),
        P(("gx", "gy", "gz"), None),
    )
    return jax.shard_map(
        shards,
        mesh=mesh,
        in_specs=placed,
        out_specs=(P(None, "gx", "gy", "gz"), P("gz", None)),
        check_vma=False,
    )
```
